32 devices in a mesh: grp: 2 (over y), chan: 4 (over z), sub: 4 (over x, core).
Axes of the slice: x: 2, y: 2, z: 4, core: 2. Of those that a mesh axis runs over, the one named last changes fastest.
Arguments:
- voltages: bfloat16 [2048, 2, 5504], P(('grp', 'chan', 'sub')), parts along dimension 0, may hold values from -6 to 6
- taps: float32 [1536], replicated, may hold values from -0.15625 to 0.15625
- input_id: int32 [1024], replicated, may hold values from 0 to 1023, each once
- counts: int32 [8], P('grp'), parts along dimension 0, may hold values from 2 to 8, as said below
- delays: int32 [512, 1024], P(('grp', 'sub')), parts along dimension 0, may hold values from 0 to 127
- beam_owner: int32 [512, 1], P('grp'), parts along dimension 0, may hold values from 0 to 3; in each aligned block of 64 rows (0 to 63, 64 to 127, ...) at most 32 rows name the same one
Outputs:
- visibility: bfloat16 [256, 2, 1024, 1024], P(('grp', 'chan'), None, 'sub'), parts along dimension 0
- resynth: float32 [1024, 2, 5504], P(('grp', 'chan', 'sub')), parts along dimension 0
The draws below stay inside these ranges and needn't reach their ends.
There are 2 independent parts, one for each index of `grp`. The reference program is written for one: setup_inputs(seed, part) draws one part's arguments, and reference() takes and returns one part's arrays. A program takes and returns all parts, laid end to end along the dimension named above; an argument that names none is the same for every part. Nothing has to cross between parts.
Inputs may be any that keep to these rules, and one draw needn't show every extreme that they name: `input_id`: each input id appears once. `counts`: every draw has a block with all 8 spectra valid. `beam_owner`: within each section of 64 consecutive beams no owner is named more than 32 times; some owner is named exactly 32 times in some section.
All inputs are finite; a program needn't handle non-finite values.
Results may differ from the reference program's by a relative error of at most 0.007.
Values may be sent and summed in bfloat16 or wider, within the bound.
No kernel may reach another device: no remote copies, remote signals or barrier semaphores. Data moves between devices by JAX's collectives and lax.ppermute only.
A program may use at most 192 MiB of HBM per device.

```python
import math
import jax
import jax.numpy as jnp
import numpy as np
from jax import lax

INPUTS = 1024
NCH = 128
TAPS = 12
SPEC = 8
BLOCKS = 4
BEAMS = 256
NSPEC = 32
SAMPLES = 5504
BEAMS_SEC = 64
MOST = 32
SLOTS = 512
N_CHAN = 4
N_SUB = 4


def draw_counts(key, part):
    lowest = max(1, SPEC // 4)
    drawn = jax.random.randint(key, (BLOCKS,), lowest, SPEC + 1)
    chosen = jax.random.randint(jax.random.fold_in(key, 7), (), 0, BLOCKS)
    return jnp.where(jnp.arange(BLOCKS) == chosen, SPEC, drawn).astype(jnp.int32)


def plant(values, key, smallest, high):
    dims = values.shape
    place = [jax.random.randint(jax.random.fold_in(key, axis), (), 0, dims[axis]) for axis in range(len(dims))]
    values = values.at[tuple(place)].set(smallest)
    longest = dims.index(max(dims))
    place[longest] = (place[longest] + 1) % dims[longest]
    return values.at[tuple(place)].set(high)


def level_of(own_key, extent, cuts, low, high):
    def one(axis_at, blocks):
        heights = jax.random.uniform(jax.random.fold_in(jax.random.fold_in(own_key, 6), axis_at), (blocks,), jnp.float32, low / len(cuts), high / len(cuts))
        return jnp.repeat(jnp.exp(heights), extent[axis_at] // blocks).reshape((-1,) + (1,) * (len(extent) - axis_at - 1))

    factor_of = one(*cuts[0])
    for cut in cuts[1:]:
        factor_of = factor_of * one(*cut)
    return factor_of


def shared_out(rng, own, number, rows, count, top, bound, skew):
    order = jax.random.permutation(rng, count)
    crowded, usual = load_shares(count, rows * top, bound, skew, True), load_shares(count, rows * top, bound, skew, False)
    places = jnp.arange(count)

    def named(tallies, rotation):
        used = int((tallies > 0).sum())
        fixed = max(1, used // 4)
        shifted = fixed + (places - fixed + rotation * (used - fixed)) % max(1, count - fixed)
        return jnp.zeros((count,), jnp.int32).at[order[jnp.where(places < fixed, places, shifted)]].set(jnp.asarray(tallies, jnp.int32))

    tallies = jnp.where(number % 4 == 0, named(crowded, number // 4), named(usual, number - number // 4 - 1))
    mixed = jax.random.permutation(jax.random.fold_in(own, 3), count)
    donor, sink = mixed[0:count // 2 * 2:2], mixed[1:count // 2 * 2:2]
    slack = jnp.minimum(tallies[donor] - 1, bound - tallies[sink]) // 2
    slack = jnp.where((donor == order[0]) | (sink == order[0]) | (tallies[sink] == 0), 0, jnp.maximum(slack, 0))
    shifted = jax.random.randint(jax.random.fold_in(own, 4), (count // 2,), 0, 1 << 20) % (slack + 1)
    tallies = tallies.at[donor].add(-shifted).at[sink].add(shifted)
    members = jnp.searchsorted(jnp.cumsum(tallies), jnp.arange(rows * top), side="right").astype(jnp.int32)
    table = members.reshape(top, rows).T
    table = table[jax.random.permutation(jax.random.fold_in(own, 1), rows)]
    rotation = jax.random.randint(jax.random.fold_in(own, 2), (rows, 1), 0, top)
    return jnp.take_along_axis(table, (jnp.arange(top)[None, :] + rotation) % top, axis=1)


def load_shares(number_of, total, bound, skew, full):
    loads = [(1 << 20) // math.isqrt(standing ** skew) + 1 for standing in range(1, number_of + 1)]
    largest = bound if full else min(bound, max(-(-total // number_of), total * loads[0] // sum(loads)))
    least = 1 if total - largest >= number_of - 1 else 0
    holding, spare = [largest] + [least] * (number_of - 1), total - largest - least * (number_of - 1)
    while spare > 0:
        candidates = [i for i in range(1, number_of) if holding[i] < largest] or [i for i in range(1, number_of) if holding[i] < bound]
        whole, left = sum([loads[i] for i in candidates]), spare
        for i in candidates:
            more = min(bound - holding[i], max(1, left * loads[i] // whole), spare)
            holding[i] = holding[i] + more
            spare = spare - more
    return np.array(holding)


def centred(stream_key, dims, deviation, most, pieces=(), held_as=jnp.bfloat16):
    loudness = level_of(stream_key, dims, pieces, -0.22, 0.18) if pieces else 1.0
    array = jax.random.normal(stream_key, dims, jnp.float32) * deviation * loudness
    return jnp.minimum(jnp.maximum(array, -most), most).astype(held_as)


def setup_inputs(seed: int = 0, part: int = 0) -> dict:
    seeds = jax.random.split(jax.random.key(seed), 7)
    own_keys = jax.random.split(jax.random.fold_in(seeds[6], part), 7)
    voltages = centred(own_keys[0], (INPUTS, 2, SAMPLES), 1.0, 6.0, ((0, 16),))
    taps = centred(seeds[1], (TAPS * NCH,), (TAPS * NCH) ** -0.5, 0.15625, (), jnp.float32)
    input_id = jax.random.permutation(seeds[2], INPUTS).astype(jnp.int32)
    counts = draw_counts(jax.random.fold_in(jax.random.fold_in(seeds[6], part), 71), part)
    delays = plant(jax.random.randint(own_keys[4], (BEAMS, INPUTS), 0, NCH), jax.random.fold_in(own_keys[4], 1), 0, NCH - 1).astype(jnp.int32)
    beam_owner_keys = jax.random.split(jax.random.fold_in(own_keys[5], 1), BEAMS // BEAMS_SEC)
    beam_owner_turns = jax.random.permutation(jax.random.fold_in(own_keys[5], 3), BEAMS // BEAMS_SEC)
    beam_owner = jax.vmap(lambda own, number: shared_out(jax.random.fold_in(own_keys[5], 2), own, number, BEAMS_SEC, N_CHAN, 1, MOST, 2))(beam_owner_keys, beam_owner_turns).reshape((BEAMS, 1))
    return dict(voltages=voltages, taps=taps, input_id=input_id, counts=counts, delays=delays, beam_owner=beam_owner)


def filter_table(taps):
    length = taps.shape[0]
    position = jnp.arange(length, dtype=jnp.int32) % NCH
    channel = jnp.arange(NCH, dtype=jnp.int32)
    phase = (position[:, None] * channel[None, :] % NCH).astype(jnp.float32) * (2.0 * math.pi / NCH)
    cosine = taps[:, None] * jnp.cos(phase)
    sine = taps[:, None] * jnp.sin(phase)
    upper = jnp.concatenate([cosine, -sine], axis=1)
    lower = jnp.concatenate([sine, cosine], axis=1)
    return jnp.concatenate([upper, lower], axis=0).astype(jnp.bfloat16)

def valid_mask(counts):
    position = jnp.arange(NSPEC, dtype=jnp.int32)
    return (position % SPEC < jnp.repeat(counts, SPEC)).astype(jnp.float32)

def channelize(volts, table, valid):
    count = volts.shape[0]
    frames = volts.reshape(count, 2, NSPEC + TAPS - 1, NCH).astype(jnp.float32)
    windows = jnp.concatenate([frames[:, :, k:k + NSPEC, :] for k in range(TAPS)], axis=3)
    table3 = table.astype(jnp.float32).reshape(2, TAPS * NCH, 2 * NCH)
    out = jnp.einsum('icth,chm->mit', windows, table3)
    out = out * valid[None, None, :]
    return out.reshape(2, NCH, count, NSPEC).astype(jnp.bfloat16)

def resynthesize(received, table):
    count = received.shape[0]
    table3 = table.astype(jnp.float32).reshape(2 * TAPS * NCH, 2, NCH)
    grid = jnp.einsum('pcht,mch->ptm', received.astype(jnp.float32), table3)
    grid = grid.reshape(count, NSPEC, 2, TAPS, NCH)
    total = jnp.zeros((count, NSPEC + TAPS - 1, 2, NCH), jnp.float32)
    for k in range(TAPS):
        total = total + jnp.pad(grid[:, :, :, k, :], ((0, 0), (k, TAPS - 1 - k), (0, 0), (0, 0)))
    return jnp.transpose(total, (0, 2, 1, 3)).reshape(count, 2, SAMPLES)

def reference(voltages, taps, input_id, counts, delays, beam_owner):
    table = filter_table(taps)
    valid = valid_mask(counts)
    total = jnp.sum(counts.astype(jnp.float32))
    group = math.gcd(64, INPUTS)
    grouped = voltages.reshape(INPUTS // group, group, 2, SAMPLES)
    parts = lax.map(lambda volts: channelize(volts, table, valid), grouped)
    spectra = jnp.transpose(parts, (1, 2, 0, 3, 4)).reshape(2, NCH, INPUTS, NSPEC)
    slot_of = jnp.zeros((INPUTS,), jnp.int32).at[input_id].set(jnp.arange(INPUTS, dtype=jnp.int32))
    by_id = jnp.take(spectra, slot_of, axis=2)
    per_channel = jnp.transpose(by_id, (1, 0, 2, 3))

    def correlate(data):
        first = data[0].astype(jnp.float32)
        second = data[1].astype(jnp.float32)
        real_part = jnp.dot(first, first.T) + jnp.dot(second, second.T)
        imag_part = jnp.dot(second, first.T) - jnp.dot(first, second.T)
        return (jnp.stack([real_part, imag_part]) / total).astype(jnp.bfloat16)
    visibility = lax.map(correlate, per_channel)

    def form(item):
        data, channel = item
        phase = (delays * channel % NCH).astype(jnp.float32) * (2.0 * math.pi / NCH)
        scale = 1.0 / math.sqrt(INPUTS)
        weight_cos = (jnp.cos(phase) * scale).astype(jnp.bfloat16).astype(jnp.float32)
        weight_sin = (jnp.sin(phase) * scale).astype(jnp.bfloat16).astype(jnp.float32)
        first = data[0].astype(jnp.float32)
        second = data[1].astype(jnp.float32)
        real_part = jnp.dot(weight_cos, first) - jnp.dot(weight_sin, second)
        imag_part = jnp.dot(weight_cos, second) + jnp.dot(weight_sin, first)
        return jnp.stack([real_part, imag_part]).astype(jnp.bfloat16)
    channels = jnp.arange(NCH, dtype=jnp.int32)
    beams = lax.map(form, (per_channel, channels))
    per_beam = jnp.transpose(beams, (2, 1, 0, 3))
    bunch = math.gcd(16, BEAMS)
    voices = lax.map(lambda rows: resynthesize(rows, table), per_beam.reshape(BEAMS // bunch, bunch, 2, NCH, NSPEC))
    voices = voices.reshape(BEAMS, 2, SAMPLES)
    owner = beam_owner[:, 0]
    beam = jnp.arange(BEAMS, dtype=jnp.int32)
    section = beam // BEAMS_SEC
    earlier = (section[:, None] == section[None, :]) & (owner[:, None] == owner[None, :]) & (beam[None, :] < beam[:, None])
    rank = lax.optimization_barrier(jnp.sum(earlier.astype(jnp.int32), axis=1)).astype(jnp.int32)
    slot = (owner * N_SUB + section) * MOST + rank
    resynth = jnp.zeros((SLOTS, 2, SAMPLES), jnp.float32).at[slot].set(voices)
    return (visibility, resynth)
```

```python
import functools
import math

import jax
import jax.numpy as jnp
from jax import lax
from jax.experimental import pallas as pl
from jax.experimental.pallas import tpu as pltpu
from jax.sharding import PartitionSpec as P

NCH = 128
TAPS = 12
SPEC = 8
BLOCKS = 4
BEAMS = 256
LANES = 128
MIB = 1024 * 1024


def filter_table(taps, chans):
    length = taps.shape[0]
    position = jnp.arange(length, dtype=jnp.int32) % chans
    channel = jnp.arange(chans, dtype=jnp.int32)
    phase = (position[:, None] * channel[None, :] % chans).astype(jnp.float32) * (
        2.0 * math.pi / chans
    )
    cosine = taps[:, None] * jnp.cos(phase)
    sine = taps[:, None] * jnp.sin(phase)
    upper = jnp.concatenate([cosine, -sine], axis=1)
    lower = jnp.concatenate([sine, cosine], axis=1)
    return jnp.concatenate([upper, lower], axis=0).astype(jnp.bfloat16)


def resynthesize(received, table, taps_count, chans):
    count = received.shape[0]
    spectra_n = received.shape[3]
    table3 = table.reshape(2 * taps_count * chans, 2, chans)
    grid = jnp.einsum("pcht,mch->ptm", received, table3, preferred_element_type=jnp.float32)
    grid = grid.reshape(count, spectra_n, 2, taps_count, chans)
    total = jnp.zeros((count, spectra_n + taps_count - 1, 2, chans), jnp.float32)
    for k in range(taps_count):
        total = total + jnp.pad(
            grid[:, :, :, k, :], ((0, 0), (k, taps_count - 1 - k), (0, 0), (0, 0))
        )
    return jnp.transpose(total, (0, 2, 1, 3)).reshape(
        count, 2, (spectra_n + taps_count - 1) * chans
    )


def general(voltages, taps, input_id, counts, delays, beam_owner):
    n_chan = lax.axis_size("chan")
    n_sub = lax.axis_size("sub")
    inp_dev = voltages.shape[0]
    inputs = input_id.shape[0]
    chans = NCH
    taps_count = TAPS
    spectra_n = BLOCKS * SPEC
    ch_dev = chans // n_chan
    rows = inputs // n_sub
    section = BEAMS // n_sub
    most = min(section, max(2, 2 * section // n_chan))
    table = filter_table(taps, chans)
    position = jnp.arange(spectra_n, dtype=jnp.int32)
    valid = (position % SPEC < jnp.repeat(counts, SPEC)).astype(jnp.float32)
    total = jnp.sum(counts.astype(jnp.float32))
    frames = voltages.reshape(inp_dev, 2, spectra_n + taps_count - 1, chans)
    windows = jnp.concatenate(
        [frames[:, :, k : k + spectra_n, :] for k in range(taps_count)], axis=3
    )
    table3 = table.reshape(2, taps_count * chans, 2 * chans)
    filtered = jnp.einsum("icth,chm->mit", windows, table3, preferred_element_type=jnp.float32)
    filtered = filtered * valid[None, None, :]
    spectra = filtered.reshape(2, chans, inp_dev, spectra_n).astype(jnp.bfloat16)
    slot_of = jnp.zeros((inputs,), jnp.int32).at[input_id].set(jnp.arange(inputs, dtype=jnp.int32))
    turned = lax.all_to_all(spectra, "chan", split_axis=1, concat_axis=2, tiled=True)
    gathered = lax.all_gather(turned, "sub", axis=2, tiled=True)
    chan_part = slot_of // (n_sub * inp_dev)
    sub_part = slot_of // inp_dev % n_sub
    order = (sub_part * n_chan + chan_part) * inp_dev + slot_of % inp_dev
    by_id = jnp.take(gathered, order, axis=2)
    sub_index = lax.axis_index("sub")
    mine = lax.dynamic_slice_in_dim(by_id, sub_index * rows, rows, 2)
    real_part = jnp.einsum("cxit,cxjt->xij", mine, by_id, preferred_element_type=jnp.float32)
    imag_part = jnp.einsum("xit,xjt->xij", mine[1], by_id[0], preferred_element_type=jnp.float32)
    imag_part = imag_part - jnp.einsum(
        "xit,xjt->xij", mine[0], by_id[1], preferred_element_type=jnp.float32
    )
    visibility = (jnp.stack([real_part, imag_part], axis=1) / total).astype(jnp.bfloat16)
    channel = lax.axis_index("chan") * ch_dev + jnp.arange(ch_dev, dtype=jnp.int32)
    phase = (delays[None, :, :] * channel[:, None, None] % chans).astype(jnp.float32) * (
        2.0 * math.pi / chans
    )
    scale = 1.0 / math.sqrt(inputs)
    weight_cos = (jnp.cos(phase) * scale).astype(jnp.bfloat16)
    weight_sin = (jnp.sin(phase) * scale).astype(jnp.bfloat16)
    from_cos = jnp.einsum("xbi,cxit->cxbt", weight_cos, by_id, preferred_element_type=jnp.float32)
    from_sin = jnp.einsum("xbi,cxit->cxbt", weight_sin, by_id, preferred_element_type=jnp.float32)
    beams = jnp.stack([from_cos[0] - from_sin[1], from_cos[1] + from_sin[0]]).astype(jnp.bfloat16)
    owner = lax.dynamic_slice_in_dim(beam_owner[:, 0], sub_index * section, section)
    beam = jnp.arange(section, dtype=jnp.int32)
    earlier = (owner[None, :] == owner[:, None]) & (beam[None, :] < beam[:, None])
    rank = jnp.sum(earlier.astype(jnp.int32), axis=1)
    target = owner * most + rank
    select = (jnp.arange(n_chan * most, dtype=jnp.int32)[:, None] == target[None, :]).astype(
        jnp.bfloat16
    )
    placed = jnp.einsum("pb,cxbt->pcxt", select, beams, preferred_element_type=jnp.float32).astype(
        jnp.bfloat16
    )
    placed = placed.reshape(n_chan, most, 2, ch_dev, spectra_n)
    resynth = resynthesize(
        lax.all_to_all(placed, "chan", split_axis=0, concat_axis=3, tiled=True)[0],
        table,
        taps_count,
        chans,
    )
    return (visibility, resynth)


def dot(a, b, dims):
    return lax.dot_general(a, b, (dims, ((), ())), preferred_element_type=jnp.float32)


def whole(shape):
    return pl.BlockSpec(shape, lambda *_: (0,) * len(shape))


SCALARS = pl.BlockSpec(memory_space=pltpu.SMEM)


def filter_kernel(inp, group, spectra_n, counts, frames, taps_col, base, *rest):
    *outs, table = rest
    depth = base.shape[0]
    for k in range(TAPS):
        table[k * depth : (k + 1) * depth, :] = (taps_col[:, k : k + 1] * base[...]).astype(
            jnp.bfloat16
        )
    width = base.shape[1] // len(outs)
    for first in range(0, spectra_n, group):
        left = jnp.concatenate(
            [
                frames[(first + k) * inp : (first + k + group) * inp, :]
                for k in range(TAPS)
            ],
            axis=1,
        )
        got = dot(left, table[...], ((1,), (0,)))
        pieces = []
        for step in range(group):
            t = first + step
            keep = (t % SPEC < counts[t // SPEC]).astype(jnp.float32)
            pieces.append(got[step * inp : (step + 1) * inp, :] * keep)
        pack = LANES // width
        for pair in range(group // pack):
            row = (first // pack + pair) * inp
            for d, out in enumerate(outs):
                out[row : row + inp, :] = jnp.concatenate(
                    [
                        pieces[pair * pack + h][:, d * width : (d + 1) * width]
                        for h in range(pack)
                    ],
                    axis=1,
                ).astype(jnp.bfloat16)


def run_filter(counts, frames, taps_col, base, inp, n_chan, spectra_n):
    width = base.shape[1] // n_chan
    pack = LANES // width
    out = jax.ShapeDtypeStruct((spectra_n // pack * inp, LANES), jnp.bfloat16)
    return pl.pallas_call(
        functools.partial(filter_kernel, inp, 4, spectra_n),
        out_shape=[out] * n_chan,
        in_specs=[SCALARS] + [pl.BlockSpec(memory_space=pltpu.VMEM)] * 3,
        out_specs=[pl.BlockSpec(memory_space=pltpu.VMEM)] * n_chan,
        scratch_shapes=[pltpu.VMEM((TAPS * base.shape[0], base.shape[1]), jnp.bfloat16)],
        compiler_params=pltpu.CompilerParams(vmem_limit_bytes=32 * MIB),
        cost_estimate=pl.CostEstimate(
            flops=2 * spectra_n * inp * TAPS * base.size,
            bytes_accessed=4 * MIB,
            transcendentals=0,
        ),
    )(counts, frames, taps_col, base)


def weight_kernel(first, delays, turn_cos, turn_sin, out):
    channel = first[0] + pl.program_id(0)
    section, inputs = delays.shape
    cosine = jnp.broadcast_to(turn_cos[0:1, :], (section, LANES))
    sine = jnp.broadcast_to(turn_sin[0:1, :], (section, LANES))
    for block in range(inputs // LANES):
        lanes = slice(block * LANES, (block + 1) * LANES)
        phase = (delays[:, lanes] * channel) & (NCH - 1)
        out[0, :section, lanes] = jnp.take_along_axis(cosine, phase, axis=1).astype(jnp.bfloat16)
        out[0, section:, lanes] = jnp.take_along_axis(sine, phase, axis=1).astype(jnp.bfloat16)


def run_weights(first, delays, turn_cos, turn_sin, ch_dev):
    section, inputs = delays.shape
    return pl.pallas_call(
        weight_kernel,
        out_shape=jax.ShapeDtypeStruct((ch_dev, 2 * section, inputs), jnp.bfloat16),
        grid=(ch_dev,),
        in_specs=[
            SCALARS,
            whole(delays.shape),
            whole(turn_cos.shape),
            whole(turn_sin.shape),
        ],
        out_specs=pl.BlockSpec((1, 2 * section, inputs), lambda f: (f, 0, 0)),
        compiler_params=pltpu.CompilerParams(vmem_limit_bytes=16 * MIB),
        cost_estimate=pl.CostEstimate(
            flops=8 * ch_dev * section * inputs,
            bytes_accessed=4 * ch_dev * section * inputs,
            transcendentals=0,
        ),
    )(first, delays, turn_cos, turn_sin)


def beam_kernel(sizes, n_blocks, n_dest, *refs):
    inp, ch_dev, spectra_n, most = sizes
    weights, choose, ids = refs[:3]
    blocks = refs[3 : 3 + n_blocks]
    by_id = refs[3 + n_blocks]
    sent = refs[4 + n_blocks : 4 + n_blocks + n_dest]
    turned, formed = refs[4 + n_blocks + n_dest :]
    channel = pl.program_id(0)
    width = 2 * ch_dev
    pack = LANES // width
    packed = spectra_n // pack
    section = weights.shape[1] // 2

    @pl.when(channel == 0)
    def _():
        together = 4
        for first in range(0, packed, together):
            left = jnp.concatenate(
                [
                    jnp.concatenate(
                        [block[t * inp : (t + 1) * inp, :] for block in blocks], axis=0
                    )
                    for t in range(first, first + together)
                ],
                axis=1,
            )
            got = dot(left, ids[...], ((0,), (0,)))
            for j in range(turned.shape[0]):
                turned[j, first * LANES : (first + together) * LANES, :] = got[
                    :, j * LANES : (j + 1) * LANES
                ]

    both = jnp.concatenate(
        [
            jnp.concatenate(
                [
                    turned[j, pl.ds(c * ch_dev + channel, spectra_n, stride=width), :]
                    for j in range(turned.shape[0])
                ],
                axis=1,
            )
            for c in range(2)
        ],
        axis=0,
    ).astype(jnp.bfloat16)
    by_id[0] = both
    got = dot(both, weights[0], ((1,), (1,)))
    real = got[:spectra_n, :section] - got[spectra_n:, section:]
    imag = got[spectra_n:, :section] + got[:spectra_n, section:]
    for c, part in enumerate((real, imag)):
        formed[pl.ds(c * ch_dev + channel, spectra_n, stride=width), :] = jnp.pad(
            part, ((0, 0), (0, LANES - section))
        )

    @pl.when(channel == ch_dev - 1)
    def _():
        per = LANES // most
        total = None
        for j in range(per):
            left = jnp.concatenate(
                [
                    formed[t * width : (t + 1) * width, :section].astype(jnp.bfloat16)
                    for t in range(j, spectra_n, per)
                ],
                axis=0,
            )
            more = dot(left, choose[j * section : (j + 1) * section, :], ((1,), (0,)))
            total = more if total is None else total + more
        for d in range(n_dest):
            sent[d][...] = total[:, d * LANES : (d + 1) * LANES].astype(jnp.bfloat16)


def run_beams(weights, choose, ids, blocks, inp, spectra_n, most, n_dest):
    ch_dev, twice, inputs = weights.shape
    width = 2 * ch_dev
    out_rows = spectra_n // (LANES // most) * width
    return pl.pallas_call(
        functools.partial(beam_kernel, (inp, ch_dev, spectra_n, most), len(blocks), n_dest),
        out_shape=[jax.ShapeDtypeStruct((ch_dev, 2 * spectra_n, inputs), jnp.bfloat16)]
        + [jax.ShapeDtypeStruct((out_rows, LANES), jnp.bfloat16)] * n_dest,
        grid=(ch_dev,),
        in_specs=[
            pl.BlockSpec((1, twice, inputs), lambda f: (f, 0, 0)),
            whole(choose.shape),
            whole(ids.shape),
        ]
        + [whole(block.shape) for block in blocks],
        out_specs=[pl.BlockSpec((1, 2 * spectra_n, inputs), lambda f: (f, 0, 0))]
        + [whole((out_rows, LANES))] * n_dest,
        scratch_shapes=[
            pltpu.VMEM((inputs // LANES, spectra_n * width, LANES), jnp.float32),
            pltpu.VMEM((spectra_n * width, LANES), jnp.float32),
        ],
        compiler_params=pltpu.CompilerParams(vmem_limit_bytes=48 * MIB),
        cost_estimate=pl.CostEstimate(
            flops=2 * spectra_n * width * inputs * inputs,
            bytes_accessed=24 * MIB,
            transcendentals=0,
        ),
    )(weights, choose, ids, *blocks)


def visibility_kernel(sub_index, counts, mine, by_id, out):
    del sub_index
    total = counts[0]
    for b in range(1, counts.shape[0]):
        total = total + counts[b]
    half = mine.shape[1] // 2
    rows = mine.shape[2]
    real, imag = mine[0, :half, :], mine[0, half:, :]
    left = jnp.concatenate(
        [jnp.concatenate([real, imag], axis=0), jnp.concatenate([imag, -real], axis=0)], axis=1
    )
    got = dot(left, by_id[0], ((0,), (0,)))
    scale = 1.0 / jnp.full((1, got.shape[1]), total, jnp.int32).astype(jnp.float32)
    out[0, 0] = (got[:rows, :] * scale).astype(jnp.bfloat16)
    out[0, 1] = (got[rows:, :] * scale).astype(jnp.bfloat16)


def run_visibility(sub_index, counts, by_id, rows):
    ch_dev, depth, inputs = by_id.shape
    return pl.pallas_call(
        visibility_kernel,
        out_shape=jax.ShapeDtypeStruct((ch_dev, 2, rows, inputs), jnp.bfloat16),
        grid_spec=pltpu.PrefetchScalarGridSpec(
            num_scalar_prefetch=2,
            grid=(ch_dev,),
            in_specs=[
                pl.BlockSpec((1, depth, rows), lambda f, sub, counts: (f, 0, sub[0])),
                pl.BlockSpec((1, depth, inputs), lambda f, sub, counts: (f, 0, 0)),
            ],
            out_specs=pl.BlockSpec((1, 2, rows, inputs), lambda f, sub, counts: (f, 0, 0, 0)),
        ),
        compiler_params=pltpu.CompilerParams(vmem_limit_bytes=24 * MIB),
        cost_estimate=pl.CostEstimate(
            flops=4 * ch_dev * depth * rows * inputs,
            bytes_accessed=4 * ch_dev * rows * inputs,
            transcendentals=0,
        ),
    )(sub_index, counts, by_id, by_id)


def resynth_kernel(most, spectra_n, taps_row, base, *refs):
    *blocks, out, table, window = refs
    depth, width = base.shape
    for k in range(TAPS):
        table[k * depth : (k + 1) * depth, :] = (taps_row[k : k + 1, :] * base[...]).astype(
            jnp.bfloat16
        )
    per = LANES // most
    edge = (TAPS - 1) * most
    window[:edge, :] = jnp.zeros((edge, depth), jnp.bfloat16)
    window[edge + spectra_n * most :, :] = jnp.zeros((edge, depth), jnp.bfloat16)
    fold = depth // len(blocks)
    for group in range(spectra_n // per):
        tall = jnp.concatenate(
            [block[group * fold : (group + 1) * fold, :] for block in blocks], axis=0
        )
        window[edge + group * LANES : edge + (group + 1) * LANES, :] = tall.T
    frames_n = spectra_n + TAPS - 1
    chans = width // 2
    step = 11
    for first in range(0, frames_n, step):
        many = min(step, frames_n - first)
        left = jnp.concatenate(
            [
                window[
                    (first + TAPS - 1 - k) * most : (first + TAPS - 1 - k + many) * most, :
                ]
                for k in range(TAPS)
            ],
            axis=1,
        )
        got = dot(left, table[...], ((1,), (0,)))
        for s in range(many):
            for c in range(2):
                out[pl.ds(2 * (first + s) + c, most, stride=2 * frames_n), :] = got[
                    s * most : (s + 1) * most, c * chans : (c + 1) * chans
                ]


def run_resynth(taps_row, base, blocks, most, spectra_n):
    frames_n = spectra_n + TAPS - 1
    return pl.pallas_call(
        functools.partial(resynth_kernel, most, spectra_n),
        out_shape=jax.ShapeDtypeStruct((most * frames_n * 2, NCH), jnp.float32),
        in_specs=[pl.BlockSpec(memory_space=pltpu.VMEM)] * (2 + len(blocks)),
        out_specs=pl.BlockSpec(memory_space=pltpu.VMEM),
        scratch_shapes=[
            pltpu.VMEM((TAPS * base.shape[0], base.shape[1]), jnp.bfloat16),
            pltpu.VMEM(((spectra_n + 2 * (TAPS - 1)) * most, base.shape[0]), jnp.bfloat16),
        ],
        compiler_params=pltpu.CompilerParams(vmem_limit_bytes=32 * MIB),
        cost_estimate=pl.CostEstimate(
            flops=2 * frames_n * most * TAPS * base.size,
            bytes_accessed=4 * MIB,
            transcendentals=0,
        ),
    )(taps_row, base, *blocks)


def swap(x, axis, size, mask):
    return lax.ppermute(x, axis, [(i, i ^ mask) for i in range(size)])


def quick(voltages, taps, input_id, counts, delays, beam_owner):
    n_chan = lax.axis_size("chan")
    n_sub = lax.axis_size("sub")
    inp = voltages.shape[0]
    inputs = input_id.shape[0]
    spectra_n = BLOCKS * SPEC
    frames_n = spectra_n + TAPS - 1
    ch_dev = NCH // n_chan
    rows = inputs // n_sub
    section = BEAMS // n_sub
    most = min(section, max(2, 2 * section // n_chan))
    chan_index = lax.axis_index("chan")
    sub_index = lax.axis_index("sub")
    turn = 2.0 * math.pi / NCH

    partner = chan_index ^ jnp.arange(n_chan, dtype=jnp.int32)
    column_channel = jnp.broadcast_to(
        (partner[:, None, None] * ch_dev + jnp.arange(ch_dev, dtype=jnp.int32)[None, None, :]),
        (n_chan, 2, ch_dev),
    ).reshape(-1)
    column_part = jnp.broadcast_to(
        jnp.arange(2, dtype=jnp.int32)[None, :, None], (n_chan, 2, ch_dev)
    ).reshape(-1)
    row_place = jnp.tile(jnp.arange(NCH, dtype=jnp.int32), 2)
    row_part = jnp.repeat(jnp.arange(2, dtype=jnp.int32), NCH)

    def fourier(place, place_part, channel, channel_part):
        quarter = (channel_part - place_part) * (NCH // 4)
        index = (place * channel + quarter + NCH) % NCH
        return jnp.cos(index.astype(jnp.float32) * turn)

    base = fourier(
        row_place[:, None], row_part[:, None], column_channel[None, :], column_part[None, :]
    )
    base_back = fourier(
        row_place[None, :], row_part[None, :], column_channel[:, None], column_part[:, None]
    )
    taps2 = taps.reshape(TAPS, NCH)
    taps_row = jnp.tile(taps2, (1, 2))
    taps_col = taps_row.T

    frames = jnp.transpose(voltages.reshape(inp, 2, frames_n, NCH), (2, 0, 1, 3)).reshape(
        frames_n * inp, 2 * NCH
    )
    outgoing = run_filter(counts, frames, taps_col, base, inp, n_chan, spectra_n)

    turned = [outgoing[0]] + [swap(outgoing[d], "chan", n_chan, d) for d in range(1, n_chan)]
    blocks = []
    for block in turned:
        held = [block]
        far = n_sub
        masks = []
        while far > 1:
            far //= 2
            masks.append(far)
        for mask in masks:
            held = held + [swap(x, "sub", n_sub, mask) for x in held]
        blocks.extend(held)
    order = [0]
    far = n_sub
    while far > 1:
        far //= 2
        order = order + [o ^ far for o in order]
    id_table = input_id.reshape(n_chan, n_sub, inp)
    slot_id = jnp.take(
        jnp.take(id_table, partner, axis=0), sub_index ^ jnp.array(order, jnp.int32), axis=1
    ).reshape(-1)
    ids = (slot_id[:, None] == jnp.arange(inputs, dtype=jnp.int32)[None, :]).astype(jnp.bfloat16)

    phases = jnp.arange(NCH, dtype=jnp.int32).astype(jnp.float32) * turn
    scale = 1.0 / math.sqrt(inputs)
    turn_cos = jnp.broadcast_to((jnp.cos(phases) * scale)[None, :], (8, NCH))
    turn_sin = jnp.broadcast_to((jnp.sin(phases) * scale)[None, :], (8, NCH))
    weights = run_weights(
        (chan_index * ch_dev).reshape(1).astype(jnp.int32), delays, turn_cos, turn_sin, ch_dev
    )

    owner = lax.dynamic_slice_in_dim(beam_owner[:, 0], sub_index * section, section)
    beam = jnp.arange(section, dtype=jnp.int32)
    earlier = (owner[None, :] == owner[:, None]) & (beam[None, :] < beam[:, None])
    rank = jnp.sum(earlier.astype(jnp.int32), axis=1)
    per = LANES // most
    line = jnp.arange(n_chan * per * most, dtype=jnp.int32)
    target = (owner ^ chan_index) * (per * most) + rank
    choose = (
        line[None, None, :]
        == target[None, :, None] + (jnp.arange(per, dtype=jnp.int32) * most)[:, None, None]
    ).astype(jnp.bfloat16).reshape(per * section, n_chan * per * most)

    by_id, *leaving = run_beams(weights, choose, ids, blocks, inp, spectra_n, most, n_chan)
    arrived = [leaving[0]] + [swap(leaving[d], "chan", n_chan, d) for d in range(1, n_chan)]
    visibility = run_visibility(
        sub_index.reshape(1).astype(jnp.int32), counts, by_id, rows
    )
    voice = run_resynth(taps_row, base_back, arrived, most, spectra_n)
    resynth = jnp.transpose(voice.reshape(most, frames_n, 2, NCH), (0, 2, 1, 3)).reshape(
        most, 2, frames_n * NCH
    )
    return (visibility, resynth)


def power_of_two(n):
    return n & (n - 1) == 0


def local(voltages, taps, input_id, counts, delays, beam_owner):
    n_chan = lax.axis_size("chan")
    n_sub = lax.axis_size("sub")
    section = BEAMS // n_sub
    most = min(section, max(2, 2 * section // n_chan))
    width = 2 * NCH // n_chan
    fits = (
        power_of_two(n_chan)
        and power_of_two(n_sub)
        and voltages.shape[0] % 16 == 0
        and LANES % width == 0
        and width % 32 == 0
        and LANES % most == 0
        and most % 16 == 0
        and section % 16 == 0
        and section <= LANES
        and input_id.shape[0] // n_sub % LANES == 0
        and (BLOCKS * SPEC) % (4 * LANES // width) == 0
    )
    form = quick if fits else general
    return form(voltages, taps, input_id, counts, delays, beam_owner)


def solution(mesh):
    placed = (
        P(("grp", "chan", "sub"), None, None),
        P(),
        P(),
        P("grp"),
        P(("grp", "sub"), None),
        P("grp", None),
    )
    return jax.shard_map(
        local,
        mesh=mesh,
        in_specs=placed,
        out_specs=(P(("grp", "chan"), None, "sub", None), P(("grp", "chan", "sub"), None, None)),
        check_vma=False,
    )
```

```python
import functools
import math

import jax
import jax.numpy as jnp
from jax import lax
from jax.experimental import pallas as pl
from jax.experimental.layout import Layout, with_layout_constraint
from jax.experimental.pallas import tpu as pltpu
from jax.sharding import PartitionSpec as P

NCH = 128
TAPS = 12
SPEC = 8
BLOCKS = 4
BEAMS = 256
LANES = 128
MIB = 1024 * 1024


def filter_table(taps, chans):
    length = taps.shape[0]
    position = jnp.arange(length, dtype=jnp.int32) % chans
    channel = jnp.arange(chans, dtype=jnp.int32)
    phase = (position[:, None] * channel[None, :] % chans).astype(jnp.float32) * (
        2.0 * math.pi / chans
    )
    cosine = taps[:, None] * jnp.cos(phase)
    sine = taps[:, None] * jnp.sin(phase)
    upper = jnp.concatenate([cosine, -sine], axis=1)
    lower = jnp.concatenate([sine, cosine], axis=1)
    return jnp.concatenate([upper, lower], axis=0).astype(jnp.bfloat16)


def resynthesize(received, table, taps_count, chans):
    count = received.shape[0]
    spectra_n = received.shape[3]
    table3 = table.reshape(2 * taps_count * chans, 2, chans)
    grid = jnp.einsum("pcht,mch->ptm", received, table3, preferred_element_type=jnp.float32)
    grid = grid.reshape(count, spectra_n, 2, taps_count, chans)
    total = jnp.zeros((count, spectra_n + taps_count - 1, 2, chans), jnp.float32)
    for k in range(taps_count):
        total = total + jnp.pad(
            grid[:, :, :, k, :], ((0, 0), (k, taps_count - 1 - k), (0, 0), (0, 0))
        )
    return jnp.transpose(total, (0, 2, 1, 3)).reshape(
        count, 2, (spectra_n + taps_count - 1) * chans
    )


def general(voltages, taps, input_id, counts, delays, beam_owner):
    n_chan = lax.axis_size("chan")
    n_sub = lax.axis_size("sub")
    inp_dev = voltages.shape[0]
    inputs = input_id.shape[0]
    chans = NCH
    taps_count = TAPS
    spectra_n = BLOCKS * SPEC
    ch_dev = chans // n_chan
    rows = inputs // n_sub
    section = BEAMS // n_sub
    most = min(section, max(2, 2 * section // n_chan))
    table = filter_table(taps, chans)
    position = jnp.arange(spectra_n, dtype=jnp.int32)
    valid = (position % SPEC < jnp.repeat(counts, SPEC)).astype(jnp.float32)
    total = jnp.sum(counts.astype(jnp.float32))
    frames = voltages.reshape(inp_dev, 2, spectra_n + taps_count - 1, chans)
    windows = jnp.concatenate(
        [frames[:, :, k : k + spectra_n, :] for k in range(taps_count)], axis=3
    )
    table3 = table.reshape(2, taps_count * chans, 2 * chans)
    filtered = jnp.einsum("icth,chm->mit", windows, table3, preferred_element_type=jnp.float32)
    filtered = filtered * valid[None, None, :]
    spectra = filtered.reshape(2, chans, inp_dev, spectra_n).astype(jnp.bfloat16)
    slot_of = jnp.zeros((inputs,), jnp.int32).at[input_id].set(jnp.arange(inputs, dtype=jnp.int32))
    turned = lax.all_to_all(spectra, "chan", split_axis=1, concat_axis=2, tiled=True)
    gathered = lax.all_gather(turned, "sub", axis=2, tiled=True)
    chan_part = slot_of // (n_sub * inp_dev)
    sub_part = slot_of // inp_dev % n_sub
    order = (sub_part * n_chan + chan_part) * inp_dev + slot_of % inp_dev
    by_id = jnp.take(gathered, order, axis=2)
    sub_index = lax.axis_index("sub")
    mine = lax.dynamic_slice_in_dim(by_id, sub_index * rows, rows, 2)
    real_part = jnp.einsum("cxit,cxjt->xij", mine, by_id, preferred_element_type=jnp.float32)
    imag_part = jnp.einsum("xit,xjt->xij", mine[1], by_id[0], preferred_element_type=jnp.float32)
    imag_part = imag_part - jnp.einsum(
        "xit,xjt->xij", mine[0], by_id[1], preferred_element_type=jnp.float32
    )
    visibility = (jnp.stack([real_part, imag_part], axis=1) / total).astype(jnp.bfloat16)
    channel = lax.axis_index("chan") * ch_dev + jnp.arange(ch_dev, dtype=jnp.int32)
    phase = (delays[None, :, :] * channel[:, None, None] % chans).astype(jnp.float32) * (
        2.0 * math.pi / chans
    )
    scale = 1.0 / math.sqrt(inputs)
    weight_cos = (jnp.cos(phase) * scale).astype(jnp.bfloat16)
    weight_sin = (jnp.sin(phase) * scale).astype(jnp.bfloat16)
    from_cos = jnp.einsum("xbi,cxit->cxbt", weight_cos, by_id, preferred_element_type=jnp.float32)
    from_sin = jnp.einsum("xbi,cxit->cxbt", weight_sin, by_id, preferred_element_type=jnp.float32)
    beams = jnp.stack([from_cos[0] - from_sin[1], from_cos[1] + from_sin[0]]).astype(jnp.bfloat16)
    owner = lax.dynamic_slice_in_dim(beam_owner[:, 0], sub_index * section, section)
    beam = jnp.arange(section, dtype=jnp.int32)
    earlier = (owner[None, :] == owner[:, None]) & (beam[None, :] < beam[:, None])
    rank = jnp.sum(earlier.astype(jnp.int32), axis=1)
    target = owner * most + rank
    select = (jnp.arange(n_chan * most, dtype=jnp.int32)[:, None] == target[None, :]).astype(
        jnp.bfloat16
    )
    placed = jnp.einsum("pb,cxbt->pcxt", select, beams, preferred_element_type=jnp.float32).astype(
        jnp.bfloat16
    )
    placed = placed.reshape(n_chan, most, 2, ch_dev, spectra_n)
    resynth = resynthesize(
        lax.all_to_all(placed, "chan", split_axis=0, concat_axis=3, tiled=True)[0],
        table,
        taps_count,
        chans,
    )
    return (visibility, resynth)


def dot(a, b, dims):
    return lax.dot_general(a, b, (dims, ((), ())), preferred_element_type=jnp.float32)


def whole(shape):
    return pl.BlockSpec(shape, lambda *_: (0,) * len(shape))


SCALARS = pl.BlockSpec(memory_space=pltpu.SMEM)


def nested(flat, pieces):
    flat = list(flat)
    out = []
    for many in pieces:
        out.append(flat[:many])
        flat = flat[many:]
    return out


def turned_by(turn_row, index):
    table = jnp.broadcast_to(turn_row, (index.shape[0], LANES))
    return jnp.concatenate(
        [
            jnp.take_along_axis(table, index[:, j : j + LANES], axis=1)
            for j in range(0, index.shape[1], LANES)
        ],
        axis=1,
    )


def filter_kernel(inp, group, spectra_n, pieces, counts, voltages, taps_col, turn_cos, index, *rest):
    *flat, table, wide, frames = rest
    outs = nested(flat, pieces)
    depth = index.shape[0]
    frames_n = spectra_n + TAPS - 1
    base = turned_by(turn_cos[0:1, :], index[...])
    for k in range(TAPS):
        table[k * depth : (k + 1) * depth, :] = (taps_col[:, k : k + 1] * base).astype(
            jnp.bfloat16
        )
    wide[...] = voltages[...].astype(jnp.float32)
    for s in range(frames_n):
        for c in range(2):
            frames[s * inp : (s + 1) * inp, c * NCH : (c + 1) * NCH] = wide[
                pl.ds(2 * s + c, inp, stride=2 * frames_n), :
            ].astype(jnp.bfloat16)
    width = index.shape[1] // len(outs)
    pack = LANES // width
    for first in range(0, spectra_n, group):
        left = jnp.concatenate(
            [
                frames[(first + k) * inp : (first + k + group) * inp, :]
                for k in range(TAPS)
            ],
            axis=1,
        )
        got = dot(left, table[...], ((1,), (0,)))
        kept = []
        for step in range(group):
            t = first + step
            keep = (t % SPEC < counts[t // SPEC]).astype(jnp.float32)
            kept.append(got[step * inp : (step + 1) * inp, :] * keep)
        for pair in range(group // pack):
            row = (first // pack + pair) * inp
            for d, parts in enumerate(outs):
                out = parts[row // parts[0].shape[0]]
                line = row % out.shape[0]
                out[line : line + inp, :] = jnp.concatenate(
                    [
                        kept[pair * pack + h][:, d * width : (d + 1) * width]
                        for h in range(pack)
                    ],
                    axis=1,
                ).astype(jnp.bfloat16)


def run_filter(counts, voltages, taps_col, turn_cos, index, inp, pieces, spectra_n):
    depth, columns = index.shape
    pack = LANES * len(pieces) // columns
    flat = pl.pallas_call(
        functools.partial(filter_kernel, inp, 4, spectra_n, pieces),
        out_shape=[
            jax.ShapeDtypeStruct((spectra_n // pack * inp // many, LANES), jnp.bfloat16)
            for many in pieces
            for _ in range(many)
        ],
        in_specs=[SCALARS] + [pl.BlockSpec(memory_space=pltpu.VMEM)] * 4,
        out_specs=[pl.BlockSpec(memory_space=pltpu.VMEM)] * sum(pieces),
        scratch_shapes=[
            pltpu.VMEM((TAPS * depth, columns), jnp.bfloat16),
            pltpu.VMEM(voltages.shape, jnp.float32),
            pltpu.VMEM((voltages.shape[0] // 2, 2 * NCH), jnp.bfloat16),
        ],
        compiler_params=pltpu.CompilerParams(vmem_limit_bytes=32 * MIB),
        cost_estimate=pl.CostEstimate(
            flops=2 * spectra_n * inp * TAPS * depth * columns,
            bytes_accessed=4 * MIB,
            transcendentals=0,
        ),
    )(counts, voltages, taps_col, turn_cos, index)
    return nested(flat, pieces)


def weight_kernel(first, delays, turn_cos, turn_sin, out):
    some = out.shape[0]
    section, inputs = delays.shape
    cosine = jnp.broadcast_to(turn_cos[0:1, :], (section, LANES))
    sine = jnp.broadcast_to(turn_sin[0:1, :], (section, LANES))
    for part in range(some):
        channel = first[0] + pl.program_id(0) * some + part
        for block in range(inputs // LANES):
            lanes = slice(block * LANES, (block + 1) * LANES)
            phase = (delays[:, lanes] * channel) & (NCH - 1)
            out[part, :section, lanes] = jnp.take_along_axis(cosine, phase, axis=1).astype(
                jnp.bfloat16
            )
            out[part, section:, lanes] = jnp.take_along_axis(sine, phase, axis=1).astype(
                jnp.bfloat16
            )


def run_weights(first, delays, turn_cos, turn_sin, ch_dev):
    section, inputs = delays.shape
    some = math.gcd(4, ch_dev)
    return pl.pallas_call(
        weight_kernel,
        out_shape=jax.ShapeDtypeStruct((ch_dev, 2 * section, inputs), jnp.bfloat16),
        grid=(ch_dev // some,),
        in_specs=[
            SCALARS,
            whole(delays.shape),
            whole(turn_cos.shape),
            whole(turn_sin.shape),
        ],
        out_specs=pl.BlockSpec((some, 2 * section, inputs), lambda f: (f, 0, 0)),
        compiler_params=pltpu.CompilerParams(vmem_limit_bytes=16 * MIB),
        cost_estimate=pl.CostEstimate(
            flops=8 * ch_dev * section * inputs,
            bytes_accessed=4 * ch_dev * section * inputs,
            transcendentals=0,
        ),
    )(first, delays, turn_cos, turn_sin)


def beam_kernel(sizes, pieces, n_dest, weights, choose, ids, *refs):
    inp, ch_dev, spectra_n, most = sizes
    blocks, refs = nested(refs[: sum(pieces)], pieces), refs[sum(pieces) :]
    by_id, sent = refs[0], refs[1 : 1 + n_dest]
    turned, formed, ordered, out_sem = refs[1 + n_dest :]
    width = 2 * ch_dev
    pitch = width + 8
    packed = spectra_n * width // LANES
    section = weights.shape[1] // 2
    n_parts = out_sem.shape[0]
    part = ch_dev // n_parts

    def store(p):
        lines = pl.ds(p * part, part)
        return pltpu.make_async_copy(ordered.at[lines], by_id.at[lines], out_sem.at[p])

    together = 4
    for first in range(0, packed, together):
        left = jnp.concatenate(
            [
                jnp.concatenate(
                    [
                        parts[t * len(parts) // packed][
                            t * inp % parts[0].shape[0] : t * inp % parts[0].shape[0] + inp, :
                        ]
                        for parts in blocks
                    ],
                    axis=0,
                )
                for t in range(first, first + together)
            ],
            axis=1,
        )
        got = dot(left, ids[...], ((0,), (0,)))
        for j in range(turned.shape[0]):
            for row in range(0, together * LANES, width):
                place = (first * LANES + row) // width * pitch
                turned[j, place : place + width, :] = got[
                    row : row + width, j * LANES : (j + 1) * LANES
                ]

    for p in range(n_parts):
        for channel in range(p * part, (p + 1) * part):
            both = jnp.concatenate(
                [
                    jnp.concatenate(
                        [
                            turned[j, pl.ds(c * ch_dev + channel, spectra_n, stride=pitch), :]
                            for j in range(turned.shape[0])
                        ],
                        axis=1,
                    )
                    for c in range(2)
                ],
                axis=0,
            ).astype(jnp.bfloat16)
            ordered[channel] = both
            got = dot(both, weights[channel], ((1,), (1,)))
            real = got[:spectra_n, :section] - got[spectra_n:, section:]
            imag = got[spectra_n:, :section] + got[:spectra_n, section:]
            for c, value in enumerate((real, imag)):
                formed[pl.ds(c * ch_dev + channel, spectra_n, stride=pitch), :] = jnp.pad(
                    value, ((0, 0), (0, LANES - section))
                )
        store(p).start()

    per = LANES // most
    total = None
    for j in range(per):
        left = jnp.concatenate(
            [
                formed[t * pitch : t * pitch + width, :section].astype(jnp.bfloat16)
                for t in range(j, spectra_n, per)
            ],
            axis=0,
        )
        more = dot(left, choose[j * section : (j + 1) * section, :], ((1,), (0,)))
        total = more if total is None else total + more
    for d in range(n_dest):
        sent[d][...] = total[:, d * LANES : (d + 1) * LANES].astype(jnp.bfloat16)
    for p in range(n_parts):
        store(p).wait()


def run_beams(weights, choose, ids, blocks, inp, spectra_n, most, n_dest):
    ch_dev, twice, inputs = weights.shape
    width = 2 * ch_dev
    out_rows = spectra_n // (LANES // most) * width
    n_parts = math.gcd(8, ch_dev)
    vmem = pl.BlockSpec(memory_space=pltpu.VMEM)
    anywhere = pl.BlockSpec(memory_space=pltpu.HBM)
    return pl.pallas_call(
        functools.partial(
            beam_kernel, (inp, ch_dev, spectra_n, most), [len(parts) for parts in blocks], n_dest
        ),
        out_shape=[jax.ShapeDtypeStruct((ch_dev, 2 * spectra_n, inputs), jnp.bfloat16)]
        + [jax.ShapeDtypeStruct((out_rows, LANES), jnp.bfloat16)] * n_dest,
        in_specs=[vmem, vmem, vmem] + [vmem] * sum(len(parts) for parts in blocks),
        out_specs=[anywhere] + [vmem] * n_dest,
        scratch_shapes=[
            pltpu.VMEM((inputs // LANES, spectra_n * (width + 8), LANES), jnp.float32),
            pltpu.VMEM((spectra_n * (width + 8), LANES), jnp.float32),
            pltpu.VMEM((ch_dev, 2 * spectra_n, inputs), jnp.bfloat16),
            pltpu.SemaphoreType.DMA((n_parts,)),
        ],
        compiler_params=pltpu.CompilerParams(vmem_limit_bytes=36 * MIB),
        cost_estimate=pl.CostEstimate(
            flops=2 * spectra_n * width * inputs * inputs,
            bytes_accessed=24 * MIB,
            transcendentals=0,
        ),
    )(weights, choose, ids, *[part for parts in blocks for part in parts])


def visibility_kernel(sub_index, counts, mine, by_id, out, held, sem):
    del sub_index
    some, depth, rows = mine.shape
    half = depth // 2
    step = pl.program_id(0)
    total = counts[0]
    for b in range(1, counts.shape[0]):
        total = total + counts[b]
    scale = 1.0 / jnp.full((1, by_id.shape[2]), total, jnp.int32).astype(jnp.float32)

    def store(part, at):
        slot = at % 2 * some + part
        return pltpu.make_async_copy(held.at[slot], out.at[at * some + part], sem.at[slot])

    @pl.when(step > 1)
    def _():
        for part in range(some):
            store(part, step - 2).wait()

    for part in range(some):
        real, imag = mine[part, :half, :], mine[part, half:, :]
        left = jnp.concatenate(
            [jnp.concatenate([real, imag], axis=0), jnp.concatenate([imag, -real], axis=0)],
            axis=1,
        )
        got = dot(left, by_id[part], ((0,), (0,)))
        slot = step % 2 * some + part
        held[slot, 0] = (got[:rows, :] * scale).astype(jnp.bfloat16)
        held[slot, 1] = (got[rows:, :] * scale).astype(jnp.bfloat16)
        store(part, step).start()

    @pl.when(step == pl.num_programs(0) - 1)
    def _():
        for before in (1, 0):

            @pl.when(step >= before)
            def _():
                for part in range(some):
                    store(part, step - before).wait()


def run_visibility(sub_index, counts, by_id, rows):
    ch_dev, depth, inputs = by_id.shape
    some = math.gcd(4, ch_dev)
    return pl.pallas_call(
        visibility_kernel,
        out_shape=jax.ShapeDtypeStruct((ch_dev, 2, rows, inputs), jnp.bfloat16),
        grid_spec=pltpu.PrefetchScalarGridSpec(
            num_scalar_prefetch=2,
            grid=(ch_dev // some,),
            in_specs=[
                pl.BlockSpec((some, depth, rows), lambda f, sub, counts: (f, 0, sub[0])),
                pl.BlockSpec((some, depth, inputs), lambda f, sub, counts: (f, 0, 0)),
            ],
            out_specs=pl.BlockSpec(memory_space=pltpu.HBM),
            scratch_shapes=[
                pltpu.VMEM((2 * some, 2, rows, inputs), jnp.bfloat16),
                pltpu.SemaphoreType.DMA((2 * some,)),
            ],
        ),
        compiler_params=pltpu.CompilerParams(vmem_limit_bytes=60 * MIB),
        cost_estimate=pl.CostEstimate(
            flops=4 * ch_dev * depth * rows * inputs,
            bytes_accessed=4 * ch_dev * rows * inputs,
            transcendentals=0,
        ),
    )(sub_index, counts, by_id, by_id)


def resynth_kernel(most, spectra_n, taps_row, turn_cos, index, *refs):
    *blocks, out, table, window = refs
    depth, width = index.shape
    base = turned_by(turn_cos[0:1, :], index[...])
    for k in range(TAPS):
        table[k * depth : (k + 1) * depth, :] = (taps_row[k : k + 1, :] * base).astype(
            jnp.bfloat16
        )
    per = LANES // most
    edge = (TAPS - 1) * most
    window[:edge, :] = jnp.zeros((edge, depth), jnp.bfloat16)
    window[edge + spectra_n * most :, :] = jnp.zeros((edge, depth), jnp.bfloat16)
    fold = depth // len(blocks)
    for group in range(spectra_n // per):
        tall = jnp.concatenate(
            [block[group * fold : (group + 1) * fold, :] for block in blocks], axis=0
        )
        window[edge + group * LANES : edge + (group + 1) * LANES, :] = tall.T
    frames_n = spectra_n + TAPS - 1
    chans = width // 2
    step = 11
    for first in range(0, frames_n, step):
        many = min(step, frames_n - first)
        left = jnp.concatenate(
            [
                window[
                    (first + TAPS - 1 - k) * most : (first + TAPS - 1 - k + many) * most, :
                ]
                for k in range(TAPS)
            ],
            axis=1,
        )
        got = dot(left, table[...], ((1,), (0,)))
        for s in range(many):
            for c in range(2):
                out[pl.ds(2 * (first + s) + c, most, stride=2 * frames_n), :] = got[
                    s * most : (s + 1) * most, c * chans : (c + 1) * chans
                ]


def run_resynth(taps_row, turn_cos, index, blocks, most, spectra_n):
    frames_n = spectra_n + TAPS - 1
    return pl.pallas_call(
        functools.partial(resynth_kernel, most, spectra_n),
        out_shape=jax.ShapeDtypeStruct((most * frames_n * 2, NCH), jnp.float32),
        in_specs=[pl.BlockSpec(memory_space=pltpu.VMEM)] * (3 + len(blocks)),
        out_specs=pl.BlockSpec(memory_space=pltpu.VMEM),
        scratch_shapes=[
            pltpu.VMEM((TAPS * index.shape[0], index.shape[1]), jnp.bfloat16),
            pltpu.VMEM(((spectra_n + 2 * (TAPS - 1)) * most, index.shape[0]), jnp.bfloat16),
        ],
        compiler_params=pltpu.CompilerParams(vmem_limit_bytes=32 * MIB),
        cost_estimate=pl.CostEstimate(
            flops=2 * frames_n * most * TAPS * index.size,
            bytes_accessed=4 * MIB,
            transcendentals=0,
        ),
    )(taps_row, turn_cos, index, *blocks)


def swap(x, axis, size, mask):
    return lax.ppermute(x, axis, [(i, i ^ mask) for i in range(size)])


def quick(voltages, taps, input_id, counts, delays, beam_owner):
    n_chan = lax.axis_size("chan")
    n_sub = lax.axis_size("sub")
    inp = voltages.shape[0]
    inputs = input_id.shape[0]
    spectra_n = BLOCKS * SPEC
    frames_n = spectra_n + TAPS - 1
    ch_dev = NCH // n_chan
    rows = inputs // n_sub
    section = BEAMS // n_sub
    most = min(section, max(2, 2 * section // n_chan))
    chan_index = lax.axis_index("chan")
    sub_index = lax.axis_index("sub")
    turn = 2.0 * math.pi / NCH

    partner = chan_index ^ jnp.arange(n_chan, dtype=jnp.int32)
    column_channel = jnp.broadcast_to(
        (partner[:, None, None] * ch_dev + jnp.arange(ch_dev, dtype=jnp.int32)[None, None, :]),
        (n_chan, 2, ch_dev),
    ).reshape(-1)
    column_part = jnp.broadcast_to(
        jnp.arange(2, dtype=jnp.int32)[None, :, None], (n_chan, 2, ch_dev)
    ).reshape(-1)
    row_place = jnp.tile(jnp.arange(NCH, dtype=jnp.int32), 2)
    row_part = jnp.repeat(jnp.arange(2, dtype=jnp.int32), NCH)

    def table_index(place, place_part, channel, channel_part):
        quarter = (channel_part - place_part) * (NCH // 4)
        return (place * channel + quarter) & (NCH - 1)

    index = table_index(
        row_place[:, None], row_part[:, None], column_channel[None, :], column_part[None, :]
    )
    index_back = table_index(
        row_place[None, :], row_part[None, :], column_channel[:, None], column_part[:, None]
    )
    phases = jnp.arange(NCH, dtype=jnp.int32).astype(jnp.float32) * turn
    turn_cos = jnp.broadcast_to(jnp.cos(phases)[None, :], (8, NCH))
    turn_sin = jnp.broadcast_to(jnp.sin(phases)[None, :], (8, NCH))
    taps_row = jnp.tile(taps.reshape(TAPS, NCH), (1, 2))
    taps_col = taps_row.T

    lines = jnp.transpose(
        with_layout_constraint(
            voltages.reshape(inp, 2, frames_n, NCH),
            Layout(major_to_minor=(0, 2, 1, 3)),
        ),
        (0, 2, 1, 3),
    ).reshape(2 * inp * frames_n, NCH)
    pieces = [1] * n_chan
    if spectra_n * ch_dev * 2 // LANES % 2 == 0:
        pieces[-1] = 1
    outgoing = run_filter(counts, lines, taps_col, turn_cos, index, inp, pieces, spectra_n)
    turned = [outgoing[0]] + [
        [swap(x, "chan", n_chan, d) for x in outgoing[d]] for d in range(1, n_chan)
    ]

    masks = []
    order = [0]
    far = n_sub
    while far > 1:
        far //= 2
        masks.append(far)
        order = order + [o ^ far for o in order]
    id_table = input_id.reshape(n_chan, n_sub, inp)
    slot_id = jnp.stack(
        [
            lax.dynamic_slice(id_table, (chan_index ^ d, sub_index ^ o, 0), (1, 1, inp))
            for d in range(n_chan)
            for o in order
        ]
    ).reshape(-1)
    scale = 1.0 / math.sqrt(inputs)
    weights = run_weights(
        (chan_index * ch_dev).reshape(1).astype(jnp.int32),
        delays,
        turn_cos * scale,
        turn_sin * scale,
        ch_dev,
    )
    turned[1][0], weights = lax.optimization_barrier((turned[1][0], weights))
    turned[0][0], slot_id = lax.optimization_barrier((turned[0][0], slot_id))
    ids = (slot_id[:, None] == jnp.arange(inputs, dtype=jnp.int32)[None, :]).astype(jnp.bfloat16)
    blocks = []
    for parts in turned:
        held = [parts]
        for mask in masks:
            held = held + [[swap(x, "sub", n_sub, mask) for x in those] for those in held]
        blocks.extend(held)

    owner = lax.dynamic_slice_in_dim(beam_owner[:, 0], sub_index * section, section)
    beam = jnp.arange(section, dtype=jnp.int32)
    earlier = (owner[None, :] == owner[:, None]) & (beam[None, :] < beam[:, None])
    rank = jnp.sum(earlier.astype(jnp.int32), axis=1)
    per = LANES // most
    line = jnp.arange(n_chan * per * most, dtype=jnp.int32)
    target = (owner ^ chan_index) * (per * most) + rank
    choose = (
        line[None, None, :]
        == target[None, :, None] + (jnp.arange(per, dtype=jnp.int32) * most)[:, None, None]
    ).astype(jnp.bfloat16).reshape(per * section, n_chan * per * most)

    by_id, *leaving = run_beams(weights, choose, ids, blocks, inp, spectra_n, most, n_chan)
    arrived = [leaving[0]] + [swap(leaving[d], "chan", n_chan, d) for d in range(1, n_chan)]
    visibility = run_visibility(
        sub_index.reshape(1).astype(jnp.int32), counts, by_id, rows
    )
    voice = run_resynth(taps_row, turn_cos, index_back, arrived, most, spectra_n)
    resynth = with_layout_constraint(
        jnp.transpose(voice.reshape(most, frames_n, 2, NCH), (0, 2, 1, 3)),
        Layout(major_to_minor=(0, 2, 1, 3)),
    ).reshape(most, 2, frames_n * NCH)
    return (visibility, resynth)


def power_of_two(n):
    return n & (n - 1) == 0


def local(voltages, taps, input_id, counts, delays, beam_owner):
    n_chan = lax.axis_size("chan")
    n_sub = lax.axis_size("sub")
    section = BEAMS // n_sub
    most = min(section, max(2, 2 * section // n_chan))
    width = 2 * NCH // n_chan
    fits = (
        power_of_two(n_chan)
        and power_of_two(n_sub)
        and voltages.shape[0] % 16 == 0
        and LANES % width == 0
        and width % 32 == 0
        and LANES % most == 0
        and most % 16 == 0
        and section % 16 == 0
        and section <= LANES
        and input_id.shape[0] // n_sub % LANES == 0
        and (BLOCKS * SPEC) % (4 * LANES // width) == 0
    )
    form = quick if fits else general
    return form(voltages, taps, input_id, counts, delays, beam_owner)


def solution(mesh):
    placed = (
        P(("grp", "chan", "sub"), None, None),
        P(),
        P(),
        P("grp"),
        P(("grp", "sub"), None),
        P("grp", None),
    )
    return jax.shard_map(
        local,
        mesh=mesh,
        in_specs=placed,
        out_specs=(P(("grp", "chan"), None, "sub", None), P(("grp", "chan", "sub"), None, None)),
        check_vma=False,
    )
```

```python
import functools
import math

import jax
import jax.numpy as jnp
from jax import lax
from jax.experimental import pallas as pl
from jax.experimental.layout import Layout, with_layout_constraint
from jax.experimental.pallas import tpu as pltpu
from jax.sharding import PartitionSpec as P

NCH = 128
TAPS = 12
SPEC = 8
BLOCKS = 4
BEAMS = 256
LANES = 128
MIB = 1024 * 1024
HALVES = 1
VIS_LIMIT = 58


def filter_table(taps, chans):
    length = taps.shape[0]
    position = jnp.arange(length, dtype=jnp.int32) % chans
    channel = jnp.arange(chans, dtype=jnp.int32)
    phase = (position[:, None] * channel[None, :] % chans).astype(jnp.float32) * (
        2.0 * math.pi / chans
    )
    cosine = taps[:, None] * jnp.cos(phase)
    sine = taps[:, None] * jnp.sin(phase)
    upper = jnp.concatenate([cosine, -sine], axis=1)
    lower = jnp.concatenate([sine, cosine], axis=1)
    return jnp.concatenate([upper, lower], axis=0).astype(jnp.bfloat16)


def resynthesize(received, table, taps_count, chans):
    count = received.shape[0]
    spectra_n = received.shape[3]
    table3 = table.reshape(2 * taps_count * chans, 2, chans)
    grid = jnp.einsum("pcht,mch->ptm", received, table3, preferred_element_type=jnp.float32)
    grid = grid.reshape(count, spectra_n, 2, taps_count, chans)
    total = jnp.zeros((count, spectra_n + taps_count - 1, 2, chans), jnp.float32)
    for k in range(taps_count):
        total = total + jnp.pad(
            grid[:, :, :, k, :], ((0, 0), (k, taps_count - 1 - k), (0, 0), (0, 0))
        )
    return jnp.transpose(total, (0, 2, 1, 3)).reshape(
        count, 2, (spectra_n + taps_count - 1) * chans
    )


def general(voltages, taps, input_id, counts, delays, beam_owner):
    n_chan = lax.axis_size("chan")
    n_sub = lax.axis_size("sub")
    inp_dev = voltages.shape[0]
    inputs = input_id.shape[0]
    chans = NCH
    taps_count = TAPS
    spectra_n = BLOCKS * SPEC
    ch_dev = chans // n_chan
    rows = inputs // n_sub
    section = BEAMS // n_sub
    most = min(section, max(2, 2 * section // n_chan))
    table = filter_table(taps, chans)
    position = jnp.arange(spectra_n, dtype=jnp.int32)
    valid = (position % SPEC < jnp.repeat(counts, SPEC)).astype(jnp.float32)
    total = jnp.sum(counts.astype(jnp.float32))
    frames = voltages.reshape(inp_dev, 2, spectra_n + taps_count - 1, chans)
    windows = jnp.concatenate(
        [frames[:, :, k : k + spectra_n, :] for k in range(taps_count)], axis=3
    )
    table3 = table.reshape(2, taps_count * chans, 2 * chans)
    filtered = jnp.einsum("icth,chm->mit", windows, table3, preferred_element_type=jnp.float32)
    filtered = filtered * valid[None, None, :]
    spectra = filtered.reshape(2, chans, inp_dev, spectra_n).astype(jnp.bfloat16)
    slot_of = jnp.zeros((inputs,), jnp.int32).at[input_id].set(jnp.arange(inputs, dtype=jnp.int32))
    turned = lax.all_to_all(spectra, "chan", split_axis=1, concat_axis=2, tiled=True)
    gathered = lax.all_gather(turned, "sub", axis=2, tiled=True)
    chan_part = slot_of // (n_sub * inp_dev)
    sub_part = slot_of // inp_dev % n_sub
    order = (sub_part * n_chan + chan_part) * inp_dev + slot_of % inp_dev
    by_id = jnp.take(gathered, order, axis=2)
    sub_index = lax.axis_index("sub")
    mine = lax.dynamic_slice_in_dim(by_id, sub_index * rows, rows, 2)
    real_part = jnp.einsum("cxit,cxjt->xij", mine, by_id, preferred_element_type=jnp.float32)
    imag_part = jnp.einsum("xit,xjt->xij", mine[1], by_id[0], preferred_element_type=jnp.float32)
    imag_part = imag_part - jnp.einsum(
        "xit,xjt->xij", mine[0], by_id[1], preferred_element_type=jnp.float32
    )
    visibility = (jnp.stack([real_part, imag_part], axis=1) / total).astype(jnp.bfloat16)
    channel = lax.axis_index("chan") * ch_dev + jnp.arange(ch_dev, dtype=jnp.int32)
    phase = (delays[None, :, :] * channel[:, None, None] % chans).astype(jnp.float32) * (
        2.0 * math.pi / chans
    )
    scale = 1.0 / math.sqrt(inputs)
    weight_cos = (jnp.cos(phase) * scale).astype(jnp.bfloat16)
    weight_sin = (jnp.sin(phase) * scale).astype(jnp.bfloat16)
    from_cos = jnp.einsum("xbi,cxit->cxbt", weight_cos, by_id, preferred_element_type=jnp.float32)
    from_sin = jnp.einsum("xbi,cxit->cxbt", weight_sin, by_id, preferred_element_type=jnp.float32)
    beams = jnp.stack([from_cos[0] - from_sin[1], from_cos[1] + from_sin[0]]).astype(jnp.bfloat16)
    owner = lax.dynamic_slice_in_dim(beam_owner[:, 0], sub_index * section, section)
    beam = jnp.arange(section, dtype=jnp.int32)
    earlier = (owner[None, :] == owner[:, None]) & (beam[None, :] < beam[:, None])
    rank = jnp.sum(earlier.astype(jnp.int32), axis=1)
    target = owner * most + rank
    select = (jnp.arange(n_chan * most, dtype=jnp.int32)[:, None] == target[None, :]).astype(
        jnp.bfloat16
    )
    placed = jnp.einsum("pb,cxbt->pcxt", select, beams, preferred_element_type=jnp.float32).astype(
        jnp.bfloat16
    )
    placed = placed.reshape(n_chan, most, 2, ch_dev, spectra_n)
    resynth = resynthesize(
        lax.all_to_all(placed, "chan", split_axis=0, concat_axis=3, tiled=True)[0],
        table,
        taps_count,
        chans,
    )
    return (visibility, resynth)


def dot(a, b, dims):
    return lax.dot_general(a, b, (dims, ((), ())), preferred_element_type=jnp.float32)


def whole(shape):
    return pl.BlockSpec(shape, lambda *_: (0,) * len(shape))


SCALARS = pl.BlockSpec(memory_space=pltpu.SMEM)


def nested(flat, pieces):
    flat = list(flat)
    out = []
    for many in pieces:
        out.append(flat[:many])
        flat = flat[many:]
    return out


def turned_by(turn_row, index):
    table = jnp.broadcast_to(turn_row, (index.shape[0], LANES))
    return jnp.concatenate(
        [
            jnp.take_along_axis(table, index[:, j : j + LANES], axis=1)
            for j in range(0, index.shape[1], LANES)
        ],
        axis=1,
    )


def filter_kernel(inp, group, spectra_n, pieces, counts, voltages, taps, turn_cos, index, *rest):
    *flat, table, wide, frames = rest
    outs = nested(flat, pieces)
    depth = index.shape[0]
    frames_n = spectra_n + TAPS - 1
    base = turned_by(turn_cos[0:1, :], index[...])
    tall = jnp.concatenate([taps[...], jnp.zeros((-TAPS % 8, NCH), jnp.float32)], axis=0).T
    tall = jnp.concatenate([tall, tall], axis=0)
    for k in range(TAPS):
        table[k * depth : (k + 1) * depth, :] = (tall[:, k : k + 1] * base).astype(
            jnp.bfloat16
        )
    wide[...] = voltages[...].astype(jnp.float32)
    for s in range(frames_n):
        for c in range(2):
            frames[s * inp : (s + 1) * inp, c * NCH : (c + 1) * NCH] = wide[
                pl.ds(2 * s + c, inp, stride=2 * frames_n), :
            ].astype(jnp.bfloat16)
    width = index.shape[1] // len(outs)
    pack = LANES // width
    for first in range(0, spectra_n, group):
        left = jnp.concatenate(
            [
                frames[(first + k) * inp : (first + k + group) * inp, :]
                for k in range(TAPS)
            ],
            axis=1,
        )
        got = dot(left, table[...], ((1,), (0,)))
        kept = []
        for step in range(group):
            t = first + step
            keep = (t % SPEC < counts[t // SPEC]).astype(jnp.float32)
            kept.append(got[step * inp : (step + 1) * inp, :] * keep)
        for pair in range(group // pack):
            row = (first // pack + pair) * inp
            for d, parts in enumerate(outs):
                out = parts[row // parts[0].shape[0]]
                line = row % out.shape[0]
                out[line : line + inp, :] = jnp.concatenate(
                    [
                        kept[pair * pack + h][:, d * width : (d + 1) * width]
                        for h in range(pack)
                    ],
                    axis=1,
                ).astype(jnp.bfloat16)


def run_filter(counts, voltages, taps, turn_cos, index, inp, pieces, spectra_n):
    depth, columns = index.shape
    pack = LANES * len(pieces) // columns
    flat = pl.pallas_call(
        functools.partial(filter_kernel, inp, 4, spectra_n, pieces),
        out_shape=[
            jax.ShapeDtypeStruct((spectra_n // pack * inp // many, LANES), jnp.bfloat16)
            for many in pieces
            for _ in range(many)
        ],
        in_specs=[SCALARS] + [pl.BlockSpec(memory_space=pltpu.VMEM)] * 4,
        out_specs=[pl.BlockSpec(memory_space=pltpu.VMEM)] * sum(pieces),
        scratch_shapes=[
            pltpu.VMEM((TAPS * depth, columns), jnp.bfloat16),
            pltpu.VMEM(voltages.shape, jnp.float32),
            pltpu.VMEM((voltages.shape[0] // 2, 2 * NCH), jnp.bfloat16),
        ],
        compiler_params=pltpu.CompilerParams(vmem_limit_bytes=36 * MIB),
        cost_estimate=pl.CostEstimate(
            flops=2 * spectra_n * inp * TAPS * depth * columns,
            bytes_accessed=4 * MIB,
            transcendentals=0,
        ),
    )(counts, voltages, taps, turn_cos, index)
    return nested(flat, pieces)


def id_matrix(order, place, input_id, ids):
    inputs = ids.shape[0]
    inp = input_id.shape[1]
    n_sub = len(order)
    line = lax.broadcasted_iota(jnp.int32, (inputs, LANES), 0)
    slots = [(d, o) for d in range(input_id.shape[0] // n_sub) for o in order]
    together = LANES // inp
    for block in range(inputs // LANES):
        carried = jnp.concatenate(
            [
                input_id[pl.ds((place[1] ^ d) * n_sub + (place[2] ^ o), 1), :]
                for d, o in slots[block * together : (block + 1) * together]
            ],
            axis=1,
        )
        ids[:, block * LANES : (block + 1) * LANES] = jnp.where(
            jnp.broadcast_to(carried, line.shape) == line, 1.0, 0.0
        ).astype(jnp.bfloat16)


def beam_kernel(sizes, order, pieces, n_dest, place, delays, turn_cos, input_id, choose, *refs):
    inp, ch_dev, spectra_n, most = sizes
    blocks, refs = nested(refs[: sum(pieces)], pieces), refs[sum(pieces) :]
    by_id, sent = refs[0], refs[1 : 1 + n_dest]
    turned, formed, ordered, ids, out_sem = refs[1 + n_dest :]
    width = 2 * ch_dev
    pitch = width + 8
    packed = spectra_n * width // LANES
    section, inputs = delays.shape
    n_parts = out_sem.shape[0]
    part = ch_dev // n_parts

    def store(p):
        lines = pl.ds(p * part, part)
        return pltpu.make_async_copy(ordered.at[lines], by_id.at[lines], out_sem.at[p])

    cosine = jnp.broadcast_to(turn_cos[0:1, :] * (1.0 / math.sqrt(inputs)), (section, LANES))
    sine = jnp.concatenate([cosine[:, -NCH // 4 :], cosine[:, : -NCH // 4]], axis=1)

    def weights(channel):
        phase = (delays[...] * (place[0] + channel)) & (NCH - 1)
        return jnp.concatenate(
            [
                jnp.concatenate(
                    [
                        jnp.take_along_axis(wave, phase[:, j : j + LANES], axis=1)
                        for j in range(0, inputs, LANES)
                    ],
                    axis=1,
                )
                for wave in (cosine, sine)
            ],
            axis=0,
        ).astype(jnp.bfloat16)

    id_matrix(order, place, input_id, ids)
    together = 4
    for first in range(0, packed, together):
        left = jnp.concatenate(
            [
                jnp.concatenate(
                    [
                        parts[t * len(parts) // packed][
                            t * inp % parts[0].shape[0] : t * inp % parts[0].shape[0] + inp, :
                        ]
                        for parts in blocks
                    ],
                    axis=0,
                )
                for t in range(first, first + together)
            ],
            axis=1,
        )
        got = dot(left, ids[...], ((0,), (1,)))
        for j in range(turned.shape[0]):
            for row in range(0, together * LANES, width):
                spot = (first * LANES + row) // width * pitch
                turned[j, spot : spot + width, :] = got[
                    row : row + width, j * LANES : (j + 1) * LANES
                ]

    for p in range(n_parts):
        for channel in range(p * part, (p + 1) * part):
            both = jnp.concatenate(
                [
                    jnp.concatenate(
                        [
                            turned[j, pl.ds(c * ch_dev + channel, spectra_n, stride=pitch), :]
                            for j in range(turned.shape[0])
                        ],
                        axis=1,
                    )
                    for c in range(2)
                ],
                axis=0,
            ).astype(jnp.bfloat16)
            ordered[channel] = both
            got = dot(both, weights(channel), ((1,), (1,)))
            real = got[:spectra_n, :section] - got[spectra_n:, section:]
            imag = got[spectra_n:, :section] + got[:spectra_n, section:]
            for c, value in enumerate((real, imag)):
                formed[pl.ds(c * ch_dev + channel, spectra_n, stride=pitch), :] = jnp.pad(
                    value, ((0, 0), (0, LANES - section))
                )
        store(p).start()

    per = LANES // most
    total = None
    for j in range(per):
        left = jnp.concatenate(
            [
                formed[t * pitch : t * pitch + width, :section].astype(jnp.bfloat16)
                for t in range(j, spectra_n, per)
            ],
            axis=0,
        )
        more = dot(left, choose[j * section : (j + 1) * section, :], ((1,), (0,)))
        total = more if total is None else total + more
    for d in range(n_dest):
        sent[d][...] = total[:, d * LANES : (d + 1) * LANES].astype(jnp.bfloat16)
    for p in range(n_parts):
        store(p).wait()


def run_beams(place, delays, turn_cos, input_id, choose, order, blocks, ch_dev, spectra_n, most, n_dest):
    section, inputs = delays.shape
    inp = input_id.shape[1]
    width = 2 * ch_dev
    out_rows = spectra_n // (LANES // most) * width
    n_parts = math.gcd(8, ch_dev)
    vmem = pl.BlockSpec(memory_space=pltpu.VMEM)
    anywhere = pl.BlockSpec(memory_space=pltpu.HBM)
    return pl.pallas_call(
        functools.partial(
            beam_kernel,
            (inp, ch_dev, spectra_n, most),
            order,
            [len(parts) for parts in blocks],
            n_dest,
        ),
        out_shape=[jax.ShapeDtypeStruct((ch_dev, 2 * spectra_n, inputs), jnp.bfloat16)]
        + [jax.ShapeDtypeStruct((out_rows, LANES), jnp.bfloat16)] * n_dest,
        in_specs=[SCALARS] + [vmem] * 4 + [vmem] * sum(len(parts) for parts in blocks),
        out_specs=[anywhere] + [vmem] * n_dest,
        scratch_shapes=[
            pltpu.VMEM((inputs // LANES, spectra_n * (width + 8), LANES), jnp.float32),
            pltpu.VMEM((spectra_n * (width + 8), LANES), jnp.float32),
            pltpu.VMEM((ch_dev, 2 * spectra_n, inputs), jnp.bfloat16),
            pltpu.VMEM((inputs, inputs), jnp.bfloat16),
            pltpu.SemaphoreType.DMA((n_parts,)),
        ],
        compiler_params=pltpu.CompilerParams(vmem_limit_bytes=46 * MIB),
        cost_estimate=pl.CostEstimate(
            flops=2 * spectra_n * width * inputs * inputs,
            bytes_accessed=24 * MIB,
            transcendentals=0,
        ),
    )(place, delays, turn_cos, input_id, choose, *[part for parts in blocks for part in parts])


def visibility_kernel(first, sub_index, counts, mine, by_id, *rest):
    *_, out, held, sem = rest
    del sub_index
    some, depth, rows = mine.shape
    half = depth // 2
    step = pl.program_id(0)
    total = counts[0]
    for b in range(1, counts.shape[0]):
        total = total + counts[b]
    scale = 1.0 / jnp.full((1, by_id.shape[2]), total, jnp.int32).astype(jnp.float32)

    def store(part, at):
        slot = at % 2 * some + part
        return pltpu.make_async_copy(held.at[slot], out.at[first + at * some + part], sem.at[slot])

    @pl.when(step > 1)
    def _():
        for part in range(some):
            store(part, step - 2).wait()

    for part in range(some):
        real, imag = mine[part, :half, :], mine[part, half:, :]
        left = jnp.concatenate(
            [jnp.concatenate([real, imag], axis=0), jnp.concatenate([imag, -real], axis=0)],
            axis=1,
        )
        got = dot(left, by_id[part], ((0,), (0,)))
        slot = step % 2 * some + part
        held[slot, 0] = (got[:rows, :] * scale).astype(jnp.bfloat16)
        held[slot, 1] = (got[rows:, :] * scale).astype(jnp.bfloat16)
        store(part, step).start()

    @pl.when(step == pl.num_programs(0) - 1)
    def _():
        for before in (1, 0):

            @pl.when(step >= before)
            def _():
                for part in range(some):
                    store(part, step - before).wait()


def run_visibility(sub_index, counts, by_id, skip, many, first, shape, before):
    depth, inputs = by_id.shape[1:]
    rows = shape[2]
    some = math.gcd(4, many)
    chained = [] if before is None else [before]
    return pl.pallas_call(
        functools.partial(visibility_kernel, first),
        out_shape=jax.ShapeDtypeStruct(shape, jnp.bfloat16),
        grid_spec=pltpu.PrefetchScalarGridSpec(
            num_scalar_prefetch=2,
            grid=(many // some,),
            in_specs=[
                pl.BlockSpec(
                    (some, depth, rows), lambda f, sub, counts: (f + skip // some, 0, sub[0])
                ),
                pl.BlockSpec(
                    (some, depth, inputs), lambda f, sub, counts: (f + skip // some, 0, 0)
                ),
            ]
            + [pl.BlockSpec(memory_space=pl.ANY) for _ in chained],
            out_specs=pl.BlockSpec(memory_space=pltpu.HBM),
            scratch_shapes=[
                pltpu.VMEM((2 * some, 2, rows, inputs), jnp.bfloat16),
                pltpu.SemaphoreType.DMA((2 * some,)),
            ],
        ),
        input_output_aliases={4: 0} if chained else {},
        compiler_params=pltpu.CompilerParams(vmem_limit_bytes=VIS_LIMIT * MIB),
        cost_estimate=pl.CostEstimate(
            flops=4 * many * depth * rows * inputs,
            bytes_accessed=4 * many * rows * inputs,
            transcendentals=0,
        ),
    )(sub_index, counts, by_id, by_id, *chained)


def resynth_kernel(most, spectra_n, taps, turn_cos, index, *refs):
    *blocks, out, table, window = refs
    depth, width = index.shape
    base = turned_by(turn_cos[0:1, :], index[...])
    wide = jnp.concatenate([taps[...], taps[...]], axis=1)
    for k in range(TAPS):
        table[k * depth : (k + 1) * depth, :] = (wide[k : k + 1, :] * base).astype(
            jnp.bfloat16
        )
    per = LANES // most
    edge = (TAPS - 1) * most
    window[:edge, :] = jnp.zeros((edge, depth), jnp.bfloat16)
    window[edge + spectra_n * most :, :] = jnp.zeros((edge, depth), jnp.bfloat16)
    fold = depth // len(blocks)
    for group in range(spectra_n // per):
        tall = jnp.concatenate(
            [block[group * fold : (group + 1) * fold, :] for block in blocks], axis=0
        )
        window[edge + group * LANES : edge + (group + 1) * LANES, :] = tall.T
    frames_n = spectra_n + TAPS - 1
    chans = width // 2
    step = 11
    for first in range(0, frames_n, step):
        many = min(step, frames_n - first)
        left = jnp.concatenate(
            [
                window[
                    (first + TAPS - 1 - k) * most : (first + TAPS - 1 - k + many) * most, :
                ]
                for k in range(TAPS)
            ],
            axis=1,
        )
        got = dot(left, table[...], ((1,), (0,)))
        for s in range(many):
            for c in range(2):
                out[pl.ds(2 * (first + s) + c, most, stride=2 * frames_n), :] = got[
                    s * most : (s + 1) * most, c * chans : (c + 1) * chans
                ]


def run_resynth(taps, turn_cos, index, blocks, most, spectra_n):
    frames_n = spectra_n + TAPS - 1
    return pl.pallas_call(
        functools.partial(resynth_kernel, most, spectra_n),
        out_shape=jax.ShapeDtypeStruct((most * frames_n * 2, NCH), jnp.float32),
        in_specs=[pl.BlockSpec(memory_space=pltpu.VMEM)] * (3 + len(blocks)),
        out_specs=pl.BlockSpec(memory_space=pltpu.VMEM),
        scratch_shapes=[
            pltpu.VMEM((TAPS * index.shape[0], index.shape[1]), jnp.bfloat16),
            pltpu.VMEM(((spectra_n + 2 * (TAPS - 1)) * most, index.shape[0]), jnp.bfloat16),
        ],
        compiler_params=pltpu.CompilerParams(vmem_limit_bytes=36 * MIB),
        cost_estimate=pl.CostEstimate(
            flops=2 * frames_n * most * TAPS * index.size,
            bytes_accessed=4 * MIB,
            transcendentals=0,
        ),
    )(taps, turn_cos, index, *blocks)


def swap(x, axis, size, mask):
    return lax.ppermute(x, axis, [(i, i ^ mask) for i in range(size)])


def quick(voltages, taps, input_id, counts, delays, beam_owner):
    n_chan = lax.axis_size("chan")
    n_sub = lax.axis_size("sub")
    inp = voltages.shape[0]
    inputs = input_id.shape[0]
    spectra_n = BLOCKS * SPEC
    frames_n = spectra_n + TAPS - 1
    ch_dev = NCH // n_chan
    rows = inputs // n_sub
    section = BEAMS // n_sub
    most = min(section, max(2, 2 * section // n_chan))
    chan_index = lax.axis_index("chan")
    sub_index = lax.axis_index("sub")
    turn = 2.0 * math.pi / NCH

    partner = chan_index ^ jnp.arange(n_chan, dtype=jnp.int32)
    ch_half = ch_dev // HALVES
    shape = (n_chan, HALVES, 2, ch_half)
    column_channel = (
        partner[:, None, None, None] * ch_dev
        + lax.broadcasted_iota(jnp.int32, shape, 1) * ch_half
        + lax.broadcasted_iota(jnp.int32, shape, 3)
    ).reshape(-1)
    column_part = lax.broadcasted_iota(jnp.int32, shape, 2).reshape(-1)
    row_place = jnp.tile(jnp.arange(NCH, dtype=jnp.int32), 2)
    row_part = jnp.repeat(jnp.arange(2, dtype=jnp.int32), NCH)

    def table_index(place, place_part, channel, channel_part):
        quarter = (channel_part - place_part) * (NCH // 4)
        return (place * channel + quarter) & (NCH - 1)

    index = table_index(
        row_place[:, None], row_part[:, None], column_channel[None, :], column_part[None, :]
    )
    index_back = table_index(
        row_place[None, :], row_part[None, :], column_channel[:, None], column_part[:, None]
    )
    phases = jnp.arange(NCH, dtype=jnp.int32).astype(jnp.float32) * turn
    turn_cos = jnp.broadcast_to(jnp.cos(phases)[None, :], (8, NCH))
    taps2 = taps.reshape(TAPS, NCH)

    lines = jnp.transpose(
        with_layout_constraint(
            voltages.reshape(inp, 2, frames_n, NCH),
            Layout(major_to_minor=(0, 2, 1, 3)),
        ),
        (0, 2, 1, 3),
    ).reshape(2 * inp * frames_n, NCH)
    outgoing = run_filter(
        counts, lines, taps2, turn_cos, index, inp, [1] * (n_chan * HALVES), spectra_n
    )
    leaving = [[outgoing[d * HALVES + h][0] for d in range(n_chan)] for h in range(HALVES)]

    masks = []
    order = [0]
    far = n_sub
    while far > 1:
        far //= 2
        masks.append(far)
        order = order + [o ^ far for o in order]
    owner = lax.dynamic_slice_in_dim(beam_owner[:, 0], sub_index * section, section)
    beam = jnp.arange(section, dtype=jnp.int32)
    earlier = (owner[None, :] == owner[:, None]) & (beam[None, :] < beam[:, None])
    rank = jnp.sum(earlier.astype(jnp.int32), axis=1)
    per = LANES // most
    line = jnp.arange(n_chan * per * most, dtype=jnp.int32)
    target = (owner ^ chan_index) * (per * most) + rank
    choose = (
        line[None, None, :]
        == target[None, :, None] + (jnp.arange(per, dtype=jnp.int32) * most)[:, None, None]
    ).astype(jnp.bfloat16).reshape(per * section, n_chan * per * most)

    id_rows = input_id.reshape(n_chan * n_sub, inp)

    def to_owners(h, d):
        return swap(leaving[h][d], "chan", n_chan, d)

    def to_all(block):
        held = [block]
        for mask in masks:
            held = held + [swap(x, "sub", n_sub, mask) for x in held]
        return [[x] for x in held]

    place = jnp.stack([chan_index * ch_dev, chan_index, sub_index]).astype(jnp.int32)

    def beams_of(arrived):
        blocks = [part for block in arrived for part in to_all(block)]
        return run_beams(
            place, delays, turn_cos, id_rows, choose, order, blocks, ch_half, spectra_n, most, n_chan
        )

    def formed_to_owners(sent):
        return [sent[0]] + [swap(sent[d], "chan", n_chan, d) for d in range(1, n_chan)]

    whole_shape = (ch_dev, 2, rows, inputs)
    sub_at = sub_index.reshape(1).astype(jnp.int32)
    partners = range(1, n_chan)

    turned = [leaving[0][0]] + [to_owners(0, d) for d in partners]
    turned[1], choose, id_rows, place = lax.optimization_barrier(
        (turned[1], choose, id_rows, place)
    )
    by_id, *sent = beams_of(turned)
    back = formed_to_owners(sent)
    visibility = run_visibility(sub_at, counts, by_id, 0, ch_dev, 0, whole_shape, None)
    voice = run_resynth(taps2, turn_cos, index_back, back, most, spectra_n)
    resynth = with_layout_constraint(
        jnp.transpose(voice.reshape(most, frames_n, 2, NCH), (0, 2, 1, 3)),
        Layout(major_to_minor=(0, 2, 1, 3)),
    ).reshape(most, 2, frames_n * NCH)
    return (visibility, resynth)


def power_of_two(n):
    return n & (n - 1) == 0


def local(voltages, taps, input_id, counts, delays, beam_owner):
    n_chan = lax.axis_size("chan")
    n_sub = lax.axis_size("sub")
    section = BEAMS // n_sub
    most = min(section, max(2, 2 * section // n_chan))
    width = 2 * NCH // n_chan // HALVES
    fits = (
        power_of_two(n_chan)
        and n_chan >= 4
        and power_of_two(n_sub)
        and voltages.shape[0] % 16 == 0
        and LANES % voltages.shape[0] == 0
        and LANES % width == 0
        and width % 16 == 0
        and width * HALVES == 2 * NCH // n_chan
        and width % 8 == 0
        and width // 2 % 8 == 0
        and LANES % most == 0
        and most % 16 == 0
        and section % 16 == 0
        and section <= LANES
        and input_id.shape[0] // n_sub % LANES == 0
        and (BLOCKS * SPEC) % (4 * LANES // width) == 0
    )
    form = quick if fits else general
    return form(voltages, taps, input_id, counts, delays, beam_owner)


def solution(mesh):
    placed = (
        P(("grp", "chan", "sub"), None, None),
        P(),
        P(),
        P("grp"),
        P(("grp", "sub"), None),
        P("grp", None),
    )
    return jax.shard_map(
        local,
        mesh=mesh,
        in_specs=placed,
        out_specs=(P(("grp", "chan"), None, "sub", None), P(("grp", "chan", "sub"), None, None)),
        check_vma=False,
    )
```

```python
import functools
import math

import jax
import jax.numpy as jnp
from jax import lax
from jax.experimental import pallas as pl
from jax.experimental.layout import Layout, with_layout_constraint
from jax.experimental.pallas import tpu as pltpu
from jax.sharding import PartitionSpec as P

NCH = 128
TAPS = 12
SPEC = 8
BLOCKS = 4
BEAMS = 256
LANES = 128
MIB = 1024 * 1024
HALVES = 1
VIS_LIMIT = 58


def filter_table(taps, chans):
    length = taps.shape[0]
    position = jnp.arange(length, dtype=jnp.int32) % chans
    channel = jnp.arange(chans, dtype=jnp.int32)
    phase = (position[:, None] * channel[None, :] % chans).astype(jnp.float32) * (
        2.0 * math.pi / chans
    )
    cosine = taps[:, None] * jnp.cos(phase)
    sine = taps[:, None] * jnp.sin(phase)
    upper = jnp.concatenate([cosine, -sine], axis=1)
    lower = jnp.concatenate([sine, cosine], axis=1)
    return jnp.concatenate([upper, lower], axis=0).astype(jnp.bfloat16)


def resynthesize(received, table, taps_count, chans):
    count = received.shape[0]
    spectra_n = received.shape[3]
    table3 = table.reshape(2 * taps_count * chans, 2, chans)
    grid = jnp.einsum("pcht,mch->ptm", received, table3, preferred_element_type=jnp.float32)
    grid = grid.reshape(count, spectra_n, 2, taps_count, chans)
    total = jnp.zeros((count, spectra_n + taps_count - 1, 2, chans), jnp.float32)
    for k in range(taps_count):
        total = total + jnp.pad(
            grid[:, :, :, k, :], ((0, 0), (k, taps_count - 1 - k), (0, 0), (0, 0))
        )
    return jnp.transpose(total, (0, 2, 1, 3)).reshape(
        count, 2, (spectra_n + taps_count - 1) * chans
    )


def general(voltages, taps, input_id, counts, delays, beam_owner):
    n_chan = lax.axis_size("chan")
    n_sub = lax.axis_size("sub")
    inp_dev = voltages.shape[0]
    inputs = input_id.shape[0]
    chans = NCH
    taps_count = TAPS
    spectra_n = BLOCKS * SPEC
    ch_dev = chans // n_chan
    rows = inputs // n_sub
    section = BEAMS // n_sub
    most = min(section, max(2, 2 * section // n_chan))
    table = filter_table(taps, chans)
    position = jnp.arange(spectra_n, dtype=jnp.int32)
    valid = (position % SPEC < jnp.repeat(counts, SPEC)).astype(jnp.float32)
    total = jnp.sum(counts.astype(jnp.float32))
    frames = voltages.reshape(inp_dev, 2, spectra_n + taps_count - 1, chans)
    windows = jnp.concatenate(
        [frames[:, :, k : k + spectra_n, :] for k in range(taps_count)], axis=3
    )
    table3 = table.reshape(2, taps_count * chans, 2 * chans)
    filtered = jnp.einsum("icth,chm->mit", windows, table3, preferred_element_type=jnp.float32)
    filtered = filtered * valid[None, None, :]
    spectra = filtered.reshape(2, chans, inp_dev, spectra_n).astype(jnp.bfloat16)
    slot_of = jnp.zeros((inputs,), jnp.int32).at[input_id].set(jnp.arange(inputs, dtype=jnp.int32))
    turned = lax.all_to_all(spectra, "chan", split_axis=1, concat_axis=2, tiled=True)
    gathered = lax.all_gather(turned, "sub", axis=2, tiled=True)
    chan_part = slot_of // (n_sub * inp_dev)
    sub_part = slot_of // inp_dev % n_sub
    order = (sub_part * n_chan + chan_part) * inp_dev + slot_of % inp_dev
    by_id = jnp.take(gathered, order, axis=2)
    sub_index = lax.axis_index("sub")
    mine = lax.dynamic_slice_in_dim(by_id, sub_index * rows, rows, 2)
    real_part = jnp.einsum("cxit,cxjt->xij", mine, by_id, preferred_element_type=jnp.float32)
    imag_part = jnp.einsum("xit,xjt->xij", mine[1], by_id[0], preferred_element_type=jnp.float32)
    imag_part = imag_part - jnp.einsum(
        "xit,xjt->xij", mine[0], by_id[1], preferred_element_type=jnp.float32
    )
    visibility = (jnp.stack([real_part, imag_part], axis=1) / total).astype(jnp.bfloat16)
    channel = lax.axis_index("chan") * ch_dev + jnp.arange(ch_dev, dtype=jnp.int32)
    phase = (delays[None, :, :] * channel[:, None, None] % chans).astype(jnp.float32) * (
        2.0 * math.pi / chans
    )
    scale = 1.0 / math.sqrt(inputs)
    weight_cos = (jnp.cos(phase) * scale).astype(jnp.bfloat16)
    weight_sin = (jnp.sin(phase) * scale).astype(jnp.bfloat16)
    from_cos = jnp.einsum("xbi,cxit->cxbt", weight_cos, by_id, preferred_element_type=jnp.float32)
    from_sin = jnp.einsum("xbi,cxit->cxbt", weight_sin, by_id, preferred_element_type=jnp.float32)
    beams = jnp.stack([from_cos[0] - from_sin[1], from_cos[1] + from_sin[0]]).astype(jnp.bfloat16)
    owner = lax.dynamic_slice_in_dim(beam_owner[:, 0], sub_index * section, section)
    beam = jnp.arange(section, dtype=jnp.int32)
    earlier = (owner[None, :] == owner[:, None]) & (beam[None, :] < beam[:, None])
    rank = jnp.sum(earlier.astype(jnp.int32), axis=1)
    target = owner * most + rank
    select = (jnp.arange(n_chan * most, dtype=jnp.int32)[:, None] == target[None, :]).astype(
        jnp.bfloat16
    )
    placed = jnp.einsum("pb,cxbt->pcxt", select, beams, preferred_element_type=jnp.float32).astype(
        jnp.bfloat16
    )
    placed = placed.reshape(n_chan, most, 2, ch_dev, spectra_n)
    resynth = resynthesize(
        lax.all_to_all(placed, "chan", split_axis=0, concat_axis=3, tiled=True)[0],
        table,
        taps_count,
        chans,
    )
    return (visibility, resynth)


def dot(a, b, dims):
    return lax.dot_general(a, b, (dims, ((), ())), preferred_element_type=jnp.float32)


def whole(shape):
    return pl.BlockSpec(shape, lambda *_: (0,) * len(shape))


SCALARS = pl.BlockSpec(memory_space=pltpu.SMEM)


def nested(flat, pieces):
    flat = list(flat)
    out = []
    for many in pieces:
        out.append(flat[:many])
        flat = flat[many:]
    return out


def turned_by(turn_row, index):
    table = jnp.broadcast_to(turn_row, (index.shape[0], LANES))
    return jnp.concatenate(
        [
            jnp.take_along_axis(table, index[:, j : j + LANES], axis=1)
            for j in range(0, index.shape[1], LANES)
        ],
        axis=1,
    )


def filter_kernel(inp, group, spectra_n, pieces, counts, voltages, taps, turn_cos, index, *rest):
    *flat, table, wide, frames, near, sem = rest
    fetch = pltpu.make_async_copy(voltages, near, sem)
    fetch.start()
    outs = nested(flat, pieces)
    depth = index.shape[0]
    frames_n = spectra_n + TAPS - 1
    base = turned_by(turn_cos[0:1, :], index[...])
    tall = jnp.concatenate([taps[...], jnp.zeros((-TAPS % 8, NCH), jnp.float32)], axis=0).T
    tall = jnp.concatenate([tall, tall], axis=0)
    for k in range(TAPS):
        table[k * depth : (k + 1) * depth, :] = (tall[:, k : k + 1] * base).astype(
            jnp.bfloat16
        )
    fetch.wait()
    wide[...] = near[...].astype(jnp.float32)
    for s in range(frames_n):
        for c in range(2):
            frames[s * inp : (s + 1) * inp, c * NCH : (c + 1) * NCH] = wide[
                pl.ds(2 * s + c, inp, stride=2 * frames_n), :
            ].astype(jnp.bfloat16)
    width = index.shape[1] // len(outs)
    pack = LANES // width
    for first in range(0, spectra_n, group):
        left = jnp.concatenate(
            [
                frames[(first + k) * inp : (first + k + group) * inp, :]
                for k in range(TAPS)
            ],
            axis=1,
        )
        got = dot(left, table[...], ((1,), (0,)))
        kept = []
        for step in range(group):
            t = first + step
            keep = (t % SPEC < counts[t // SPEC]).astype(jnp.float32)
            kept.append(got[step * inp : (step + 1) * inp, :] * keep)
        for pair in range(group // pack):
            row = (first // pack + pair) * inp
            for d, parts in enumerate(outs):
                out = parts[row // parts[0].shape[0]]
                line = row % out.shape[0]
                out[line : line + inp, :] = jnp.concatenate(
                    [
                        kept[pair * pack + h][:, d * width : (d + 1) * width]
                        for h in range(pack)
                    ],
                    axis=1,
                ).astype(jnp.bfloat16)


def run_filter(counts, voltages, taps, turn_cos, index, inp, pieces, spectra_n):
    depth, columns = index.shape
    pack = LANES * len(pieces) // columns
    flat = pl.pallas_call(
        functools.partial(filter_kernel, inp, 4, spectra_n, pieces),
        out_shape=[
            jax.ShapeDtypeStruct((spectra_n // pack * inp // many, LANES), jnp.bfloat16)
            for many in pieces
            for _ in range(many)
        ],
        in_specs=[SCALARS, pl.BlockSpec(memory_space=pltpu.HBM)]
        + [pl.BlockSpec(memory_space=pltpu.VMEM)] * 3,
        out_specs=[pl.BlockSpec(memory_space=pltpu.VMEM)] * sum(pieces),
        scratch_shapes=[
            pltpu.VMEM((TAPS * depth, columns), jnp.bfloat16),
            pltpu.VMEM(voltages.shape, jnp.float32),
            pltpu.VMEM((voltages.shape[0] // 2, 2 * NCH), jnp.bfloat16),
            pltpu.VMEM(voltages.shape, jnp.bfloat16),
            pltpu.SemaphoreType.DMA,
        ],
        compiler_params=pltpu.CompilerParams(vmem_limit_bytes=36 * MIB),
        cost_estimate=pl.CostEstimate(
            flops=2 * spectra_n * inp * TAPS * depth * columns,
            bytes_accessed=4 * MIB,
            transcendentals=0,
        ),
    )(counts, voltages, taps, turn_cos, index)
    return nested(flat, pieces)


def id_matrix(order, place, input_id, ids):
    inputs = ids.shape[0]
    inp = input_id.shape[1]
    n_sub = len(order)
    line = lax.broadcasted_iota(jnp.int32, (inputs, LANES), 0)
    slots = [(d, o) for d in range(input_id.shape[0] // n_sub) for o in order]
    together = LANES // inp
    for block in range(inputs // LANES):
        carried = jnp.concatenate(
            [
                input_id[pl.ds((place[1] ^ d) * n_sub + (place[2] ^ o), 1), :]
                for d, o in slots[block * together : (block + 1) * together]
            ],
            axis=1,
        )
        ids[:, block * LANES : (block + 1) * LANES] = jnp.where(
            jnp.broadcast_to(carried, line.shape) == line, 1.0, 0.0
        ).astype(jnp.bfloat16)


def beam_kernel(sizes, order, pieces, n_dest, place, delays, turn_cos, input_id, choose, *refs):
    inp, ch_dev, spectra_n, most = sizes
    blocks, refs = nested(refs[: sum(pieces)], pieces), refs[sum(pieces) :]
    by_id, sent = refs[0], refs[1 : 1 + n_dest]
    turned, formed, ordered, ids, out_sem = refs[1 + n_dest :]
    width = 2 * ch_dev
    pitch = width + 8
    packed = spectra_n * width // LANES
    section, inputs = delays.shape
    n_parts = out_sem.shape[0]
    part = ch_dev // n_parts

    def store(p):
        lines = pl.ds(p * part, part)
        return pltpu.make_async_copy(ordered.at[lines], by_id.at[lines], out_sem.at[p])

    cosine = jnp.broadcast_to(turn_cos[0:1, :] * (1.0 / math.sqrt(inputs)), (section, LANES))
    sine = jnp.concatenate([cosine[:, -NCH // 4 :], cosine[:, : -NCH // 4]], axis=1)

    def weights(channel):
        phase = (delays[...] * (place[0] + channel)) & (NCH - 1)
        return jnp.concatenate(
            [
                jnp.concatenate(
                    [
                        jnp.take_along_axis(wave, phase[:, j : j + LANES], axis=1)
                        for j in range(0, inputs, LANES)
                    ],
                    axis=1,
                )
                for wave in (cosine, sine)
            ],
            axis=0,
        ).astype(jnp.bfloat16)

    id_matrix(order, place, input_id, ids)
    together = 4
    for first in range(0, packed, together):
        left = jnp.concatenate(
            [
                jnp.concatenate(
                    [
                        parts[t * len(parts) // packed][
                            t * inp % parts[0].shape[0] : t * inp % parts[0].shape[0] + inp, :
                        ]
                        for parts in blocks
                    ],
                    axis=0,
                )
                for t in range(first, first + together)
            ],
            axis=1,
        )
        got = dot(left, ids[...], ((0,), (1,)))
        for j in range(turned.shape[0]):
            for row in range(0, together * LANES, width):
                spot = (first * LANES + row) // width * pitch
                turned[j, spot : spot + width, :] = got[
                    row : row + width, j * LANES : (j + 1) * LANES
                ]

    for p in range(n_parts):
        for channel in range(p * part, (p + 1) * part):
            both = jnp.concatenate(
                [
                    jnp.concatenate(
                        [
                            turned[j, pl.ds(c * ch_dev + channel, spectra_n, stride=pitch), :]
                            for j in range(turned.shape[0])
                        ],
                        axis=1,
                    )
                    for c in range(2)
                ],
                axis=0,
            ).astype(jnp.bfloat16)
            ordered[channel] = both
            got = dot(both, weights(channel), ((1,), (1,)))
            real = got[:spectra_n, :section] - got[spectra_n:, section:]
            imag = got[spectra_n:, :section] + got[:spectra_n, section:]
            for c, value in enumerate((real, imag)):
                formed[pl.ds(c * ch_dev + channel, spectra_n, stride=pitch), :] = jnp.pad(
                    value, ((0, 0), (0, LANES - section))
                )
        store(p).start()

    per = LANES // most
    total = None
    for j in range(per):
        left = jnp.concatenate(
            [
                formed[t * pitch : t * pitch + width, :section].astype(jnp.bfloat16)
                for t in range(j, spectra_n, per)
            ],
            axis=0,
        )
        more = dot(left, choose[j * section : (j + 1) * section, :], ((1,), (0,)))
        total = more if total is None else total + more
    for d in range(n_dest):
        sent[d][...] = total[:, d * LANES : (d + 1) * LANES].astype(jnp.bfloat16)
    for p in range(n_parts):
        store(p).wait()


def run_beams(place, delays, turn_cos, input_id, choose, order, blocks, ch_dev, spectra_n, most, n_dest):
    section, inputs = delays.shape
    inp = input_id.shape[1]
    width = 2 * ch_dev
    out_rows = spectra_n // (LANES // most) * width
    n_parts = math.gcd(8, ch_dev)
    vmem = pl.BlockSpec(memory_space=pltpu.VMEM)
    anywhere = pl.BlockSpec(memory_space=pltpu.HBM)
    return pl.pallas_call(
        functools.partial(
            beam_kernel,
            (inp, ch_dev, spectra_n, most),
            order,
            [len(parts) for parts in blocks],
            n_dest,
        ),
        out_shape=[jax.ShapeDtypeStruct((ch_dev, 2 * spectra_n, inputs), jnp.bfloat16)]
        + [jax.ShapeDtypeStruct((out_rows, LANES), jnp.bfloat16)] * n_dest,
        in_specs=[SCALARS] + [vmem] * 4 + [vmem] * sum(len(parts) for parts in blocks),
        out_specs=[anywhere] + [vmem] * n_dest,
        scratch_shapes=[
            pltpu.VMEM((inputs // LANES, spectra_n * (width + 8), LANES), jnp.float32),
            pltpu.VMEM((spectra_n * (width + 8), LANES), jnp.float32),
            pltpu.VMEM((ch_dev, 2 * spectra_n, inputs), jnp.bfloat16),
            pltpu.VMEM((inputs, inputs), jnp.bfloat16),
            pltpu.SemaphoreType.DMA((n_parts,)),
        ],
        compiler_params=pltpu.CompilerParams(vmem_limit_bytes=46 * MIB),
        cost_estimate=pl.CostEstimate(
            flops=2 * spectra_n * width * inputs * inputs,
            bytes_accessed=24 * MIB,
            transcendentals=0,
        ),
    )(place, delays, turn_cos, input_id, choose, *[part for parts in blocks for part in parts])


def visibility_kernel(first, sub_index, counts, mine, by_id, *rest):
    *_, out, held, sem = rest
    del sub_index
    some, depth, rows = mine.shape
    half = depth // 2
    step = pl.program_id(0)
    total = counts[0]
    for b in range(1, counts.shape[0]):
        total = total + counts[b]
    scale = 1.0 / jnp.full((1, by_id.shape[2]), total, jnp.int32).astype(jnp.float32)

    def store(part, at):
        slot = at % 2 * some + part
        return pltpu.make_async_copy(held.at[slot], out.at[first + at * some + part], sem.at[slot])

    @pl.when(step > 1)
    def _():
        for part in range(some):
            store(part, step - 2).wait()

    for part in range(some):
        real, imag = mine[part, :half, :], mine[part, half:, :]
        left = jnp.concatenate(
            [jnp.concatenate([real, imag], axis=0), jnp.concatenate([imag, -real], axis=0)],
            axis=1,
        )
        got = dot(left, by_id[part], ((0,), (0,)))
        slot = step % 2 * some + part
        held[slot, 0] = (got[:rows, :] * scale).astype(jnp.bfloat16)
        held[slot, 1] = (got[rows:, :] * scale).astype(jnp.bfloat16)
        store(part, step).start()

    @pl.when(step == pl.num_programs(0) - 1)
    def _():
        for before in (1, 0):

            @pl.when(step >= before)
            def _():
                for part in range(some):
                    store(part, step - before).wait()


def run_visibility(sub_index, counts, by_id, skip, many, first, shape, before):
    depth, inputs = by_id.shape[1:]
    rows = shape[2]
    some = math.gcd(4, many)
    chained = [] if before is None else [before]
    return pl.pallas_call(
        functools.partial(visibility_kernel, first),
        out_shape=jax.ShapeDtypeStruct(shape, jnp.bfloat16),
        grid_spec=pltpu.PrefetchScalarGridSpec(
            num_scalar_prefetch=2,
            grid=(many // some,),
            in_specs=[
                pl.BlockSpec(
                    (some, depth, rows), lambda f, sub, counts: (f + skip // some, 0, sub[0])
                ),
                pl.BlockSpec(
                    (some, depth, inputs), lambda f, sub, counts: (f + skip // some, 0, 0)
                ),
            ]
            + [pl.BlockSpec(memory_space=pl.ANY) for _ in chained],
            out_specs=pl.BlockSpec(memory_space=pltpu.HBM),
            scratch_shapes=[
                pltpu.VMEM((2 * some, 2, rows, inputs), jnp.bfloat16),
                pltpu.SemaphoreType.DMA((2 * some,)),
            ],
        ),
        input_output_aliases={4: 0} if chained else {},
        compiler_params=pltpu.CompilerParams(vmem_limit_bytes=VIS_LIMIT * MIB),
        cost_estimate=pl.CostEstimate(
            flops=4 * many * depth * rows * inputs,
            bytes_accessed=4 * many * rows * inputs,
            transcendentals=0,
        ),
    )(sub_index, counts, by_id, by_id, *chained)


def resynth_kernel(most, spectra_n, taps, turn_cos, index, *refs):
    *blocks, out, table, window = refs
    depth, width = index.shape
    base = turned_by(turn_cos[0:1, :], index[...])
    wide = jnp.concatenate([taps[...], taps[...]], axis=1)
    for k in range(TAPS):
        table[k * depth : (k + 1) * depth, :] = (wide[k : k + 1, :] * base).astype(
            jnp.bfloat16
        )
    per = LANES // most
    edge = (TAPS - 1) * most
    window[:edge, :] = jnp.zeros((edge, depth), jnp.bfloat16)
    window[edge + spectra_n * most :, :] = jnp.zeros((edge, depth), jnp.bfloat16)
    fold = depth // len(blocks)
    for group in range(spectra_n // per):
        tall = jnp.concatenate(
            [block[group * fold : (group + 1) * fold, :] for block in blocks], axis=0
        )
        window[edge + group * LANES : edge + (group + 1) * LANES, :] = tall.T
    frames_n = spectra_n + TAPS - 1
    chans = width // 2
    step = 11
    for first in range(0, frames_n, step):
        many = min(step, frames_n - first)
        left = jnp.concatenate(
            [
                window[
                    (first + TAPS - 1 - k) * most : (first + TAPS - 1 - k + many) * most, :
                ]
                for k in range(TAPS)
            ],
            axis=1,
        )
        got = dot(left, table[...], ((1,), (0,)))
        for s in range(many):
            for c in range(2):
                out[pl.ds(2 * (first + s) + c, most, stride=2 * frames_n), :] = got[
                    s * most : (s + 1) * most, c * chans : (c + 1) * chans
                ]


def run_resynth(taps, turn_cos, index, blocks, most, spectra_n):
    frames_n = spectra_n + TAPS - 1
    return pl.pallas_call(
        functools.partial(resynth_kernel, most, spectra_n),
        out_shape=jax.ShapeDtypeStruct((most * frames_n * 2, NCH), jnp.float32),
        in_specs=[pl.BlockSpec(memory_space=pltpu.VMEM)] * (3 + len(blocks)),
        out_specs=pl.BlockSpec(memory_space=pltpu.VMEM),
        scratch_shapes=[
            pltpu.VMEM((TAPS * index.shape[0], index.shape[1]), jnp.bfloat16),
            pltpu.VMEM(((spectra_n + 2 * (TAPS - 1)) * most, index.shape[0]), jnp.bfloat16),
        ],
        compiler_params=pltpu.CompilerParams(vmem_limit_bytes=36 * MIB),
        cost_estimate=pl.CostEstimate(
            flops=2 * frames_n * most * TAPS * index.size,
            bytes_accessed=4 * MIB,
            transcendentals=0,
        ),
    )(taps, turn_cos, index, *blocks)


def swap(x, axis, size, mask):
    return lax.ppermute(x, axis, [(i, i ^ mask) for i in range(size)])


def quick(voltages, taps, input_id, counts, delays, beam_owner):
    n_chan = lax.axis_size("chan")
    n_sub = lax.axis_size("sub")
    inp = voltages.shape[0]
    inputs = input_id.shape[0]
    spectra_n = BLOCKS * SPEC
    frames_n = spectra_n + TAPS - 1
    ch_dev = NCH // n_chan
    rows = inputs // n_sub
    section = BEAMS // n_sub
    most = min(section, max(2, 2 * section // n_chan))
    chan_index = lax.axis_index("chan")
    sub_index = lax.axis_index("sub")
    turn = 2.0 * math.pi / NCH

    partner = chan_index ^ jnp.arange(n_chan, dtype=jnp.int32)
    ch_half = ch_dev // HALVES
    shape = (n_chan, HALVES, 2, ch_half)
    column_channel = (
        partner[:, None, None, None] * ch_dev
        + lax.broadcasted_iota(jnp.int32, shape, 1) * ch_half
        + lax.broadcasted_iota(jnp.int32, shape, 3)
    ).reshape(-1)
    column_part = lax.broadcasted_iota(jnp.int32, shape, 2).reshape(-1)
    row_place = jnp.tile(jnp.arange(NCH, dtype=jnp.int32), 2)
    row_part = jnp.repeat(jnp.arange(2, dtype=jnp.int32), NCH)

    def table_index(place, place_part, channel, channel_part):
        quarter = (channel_part - place_part) * (NCH // 4)
        return (place * channel + quarter) & (NCH - 1)

    index = table_index(
        row_place[:, None], row_part[:, None], column_channel[None, :], column_part[None, :]
    )
    index_back = table_index(
        row_place[None, :], row_part[None, :], column_channel[:, None], column_part[:, None]
    )
    phases = jnp.arange(NCH, dtype=jnp.int32).astype(jnp.float32) * turn
    turn_cos = jnp.broadcast_to(jnp.cos(phases)[None, :], (8, NCH))
    taps2 = taps.reshape(TAPS, NCH)

    lines = jnp.transpose(
        with_layout_constraint(
            voltages.reshape(inp, 2, frames_n, NCH),
            Layout(major_to_minor=(0, 2, 1, 3)),
        ),
        (0, 2, 1, 3),
    ).reshape(2 * inp * frames_n, NCH)
    outgoing = run_filter(
        counts, lines, taps2, turn_cos, index, inp, [1] * (n_chan * HALVES), spectra_n
    )
    leaving = [[outgoing[d * HALVES + h][0] for d in range(n_chan)] for h in range(HALVES)]

    masks = []
    order = [0]
    far = n_sub
    while far > 1:
        far //= 2
        masks.append(far)
        order = order + [o ^ far for o in order]
    owner = lax.dynamic_slice_in_dim(beam_owner[:, 0], sub_index * section, section)
    beam = jnp.arange(section, dtype=jnp.int32)
    earlier = (owner[None, :] == owner[:, None]) & (beam[None, :] < beam[:, None])
    rank = jnp.sum(earlier.astype(jnp.int32), axis=1)
    per = LANES // most
    line = jnp.arange(n_chan * per * most, dtype=jnp.int32)
    target = (owner ^ chan_index) * (per * most) + rank
    choose = (
        line[None, None, :]
        == target[None, :, None] + (jnp.arange(per, dtype=jnp.int32) * most)[:, None, None]
    ).astype(jnp.bfloat16).reshape(per * section, n_chan * per * most)

    id_rows = input_id.reshape(n_chan * n_sub, inp)

    def to_owners(h, d):
        return swap(leaving[h][d], "chan", n_chan, d)

    def to_all(block):
        held = [block]
        for mask in masks:
            held = held + [swap(x, "sub", n_sub, mask) for x in held]
        return [[x] for x in held]

    place = jnp.stack([chan_index * ch_dev, chan_index, sub_index]).astype(jnp.int32)

    def beams_of(arrived):
        blocks = [part for block in arrived for part in to_all(block)]
        return run_beams(
            place, delays, turn_cos, id_rows, choose, order, blocks, ch_half, spectra_n, most, n_chan
        )

    def formed_to_owners(sent):
        return [sent[0]] + [swap(sent[d], "chan", n_chan, d) for d in range(1, n_chan)]

    whole_shape = (ch_dev, 2, rows, inputs)
    sub_at = sub_index.reshape(1).astype(jnp.int32)
    partners = range(1, n_chan)

    turned = [leaving[0][0]] + [to_owners(0, d) for d in partners]
    turned[1], choose, id_rows, place = lax.optimization_barrier(
        (turned[1], choose, id_rows, place)
    )
    by_id, *sent = beams_of(turned)
    back = formed_to_owners(sent)
    visibility = run_visibility(sub_at, counts, by_id, 0, ch_dev, 0, whole_shape, None)
    voice = run_resynth(taps2, turn_cos, index_back, back, most, spectra_n)
    resynth = with_layout_constraint(
        jnp.transpose(voice.reshape(most, frames_n, 2, NCH), (0, 2, 1, 3)),
        Layout(major_to_minor=(0, 2, 1, 3)),
    ).reshape(most, 2, frames_n * NCH)
    return (visibility, resynth)


def power_of_two(n):
    return n & (n - 1) == 0


def local(voltages, taps, input_id, counts, delays, beam_owner):
    n_chan = lax.axis_size("chan")
    n_sub = lax.axis_size("sub")
    section = BEAMS // n_sub
    most = min(section, max(2, 2 * section // n_chan))
    width = 2 * NCH // n_chan // HALVES
    fits = (
        power_of_two(n_chan)
        and n_chan >= 4
        and power_of_two(n_sub)
        and voltages.shape[0] % 16 == 0
        and LANES % voltages.shape[0] == 0
        and LANES % width == 0
        and width % 16 == 0
        and width * HALVES == 2 * NCH // n_chan
        and width % 8 == 0
        and width // 2 % 8 == 0
        and LANES % most == 0
        and most % 16 == 0
        and section % 16 == 0
        and section <= LANES
        and input_id.shape[0] // n_sub % LANES == 0
        and (BLOCKS * SPEC) % (4 * LANES // width) == 0
    )
    form = quick if fits else general
    return form(voltages, taps, input_id, counts, delays, beam_owner)


def solution(mesh):
    placed = (
        P(("grp", "chan", "sub"), None, None),
        P(),
        P(),
        P("grp"),
        P(("grp", "sub"), None),
        P("grp", None),
    )
    return jax.shard_map(
        local,
        mesh=mesh,
        in_specs=placed,
        out_specs=(P(("grp", "chan"), None, "sub", None), P(("grp", "chan", "sub"), None, None)),
        check_vma=False,
    )
```
